512 devices in a mesh: row: 16 (over y, x), col: 32 (over z, core).
Axes of the slice: x: 4, y: 4, z: 16, core: 2. Of those that a mesh axis runs over, the one named last changes fastest.
Arguments:
- src_feat: bfloat16 [64, 65536], P(None, ('row', 'col')), may hold values from -1 to 1
- tgt_feat: bfloat16 [64, 32768], P(None, 'col'), may hold values from -1 to 1
Outputs:
- src_potential: float32 [65536], P('row')
- tgt_potential: float32 [32768], P('col')
The draws below stay inside these ranges and needn't reach their ends.
All inputs are finite; a program needn't handle non-finite values.
Results may differ from the reference program's by a relative error of at most 0.0003.
Values may be sent and summed in bfloat16 or wider, within the bound.
No kernel may reach another device: no remote copies, remote signals or barrier semaphores. Data moves between devices by JAX's collectives and lax.ppermute only.
A program may use at most 64 MiB of HBM per device.

```python
import math
import jax
import jax.numpy as jnp
from jax import lax

F = 64
ITERS = 2
SOURCES = 65536
TARGETS = 32768


def draw_points(key, count):
    first = jax.random.fold_in(key, 0)
    base = jnp.clip(jax.random.normal(first, (F, count), jnp.float32), -6.0, 6.0) * 0.125
    return base.astype(jnp.bfloat16)


def draw_src_feat(key, part):
    key = jax.random.fold_in(key, 11)
    return draw_points(key, SOURCES)


def draw_tgt_feat(key, part):
    key = jax.random.fold_in(key, 23)
    return draw_points(key, TARGETS)


def setup_inputs(seed: int = 0) -> dict:
    streams_of = jax.random.split(jax.random.key(seed), 3)
    return {
        "src_feat": draw_src_feat(jax.random.fold_in(streams_of[2], 71), 0),
        "tgt_feat": draw_tgt_feat(jax.random.fold_in(streams_of[2], 71), 0),
    }


INV_EPS = 20.0
EPS = 0.05


def pair_costs(xs, xsq, ys, ysq):
    inner = jnp.dot(xs.T, ys, preferred_element_type=jnp.float32)
    return (xsq[:, None] + ysq[None, :]) - 2.0 * inner


def reference(src_feat, tgt_feat):
    src_sq = jnp.sum(jnp.square(src_feat.astype(jnp.float32)), axis=0)
    tgt_sq = jnp.sum(jnp.square(tgt_feat.astype(jnp.float32)), axis=0)
    src_size = min(512, SOURCES)
    tgt_size = min(512, TARGETS)
    src_blocks = src_feat.reshape(F, SOURCES // src_size, src_size).transpose(1, 0, 2)
    src_sq_blocks = src_sq.reshape(SOURCES // src_size, src_size)
    tgt_blocks = tgt_feat.reshape(F, TARGETS // tgt_size, tgt_size).transpose(1, 0, 2)
    tgt_sq_blocks = tgt_sq.reshape(TARGETS // tgt_size, tgt_size)
    tgt_pot = jnp.zeros((TARGETS,), jnp.float32)
    src_pot = jnp.zeros((SOURCES,), jnp.float32)
    for step in range(ITERS):
        def row_block(args):
            feats, sq = args
            scores = (tgt_pot[None, :] - pair_costs(feats, sq, tgt_feat, tgt_sq)) * INV_EPS
            peak = jnp.max(scores, axis=1)
            return peak + jnp.log(jnp.sum(jnp.exp(scores - peak[:, None]), axis=1))

        row_lse = lax.map(row_block, (src_blocks, src_sq_blocks)).reshape(SOURCES)
        src_pot = -EPS * (row_lse - math.log(TARGETS))

        def col_block(args):
            feats, sq = args
            scores = (src_pot[:, None] - pair_costs(src_feat, src_sq, feats, sq)) * INV_EPS
            peak = jnp.max(scores, axis=0)
            return peak + jnp.log(jnp.sum(jnp.exp(scores - peak[None, :]), axis=0))

        col_lse = lax.map(col_block, (tgt_blocks, tgt_sq_blocks)).reshape(TARGETS)
        tgt_pot = -EPS * (col_lse - math.log(SOURCES))
    return src_pot, tgt_pot
```

```python
import math

import jax
import jax.numpy as jnp
from jax import lax
from jax.sharding import Mesh, PartitionSpec as P

ITERS = 2
INV_EPS = 20.0
EPS = 0.05
BLOCK = 512


def squares(feats):
    return jnp.sum(jnp.square(feats.astype(jnp.float32)), axis=-2)


def share(value, axis, size):
    spread = jnp.broadcast_to(value[None], (size,) + value.shape)
    return lax.all_to_all(spread, axis, 0, 0, tiled=False)


def merge(parts):
    peak = jnp.max(parts, axis=0)
    return peak + jnp.log(jnp.sum(jnp.exp(parts - peak[None]), axis=0))


def partial_lse(over, over_sq, over_pot, kept, kept_sq):
    def one(args):
        feats, sq, pot = args
        inner = lax.dot_general(feats, kept, (((0,), (0,)), ((), ())), preferred_element_type=jnp.float32)
        scores = (pot[:, None] - ((sq[:, None] + kept_sq[None, :]) - 2.0 * inner)) * INV_EPS
        peak = jnp.max(scores, axis=0)
        return peak, jnp.sum(jnp.exp(scores - peak[None, :]), axis=0)

    peaks, totals = lax.map(one, (over, over_sq, over_pot))
    peak = jnp.max(peaks, axis=0)
    return peak + jnp.log(jnp.sum(totals * jnp.exp(peaks - peak[None]), axis=0))


def per_device(n_row, n_z, n_core, src_feat, tgt_feat):
    sources = src_feat.shape[1] * n_row * n_z * n_core
    targets = tgt_feat.shape[1] * n_z * n_core
    width, tgt_own = tgt_feat.shape
    tgt = lax.all_gather(tgt_feat, "core")
    src = share(src_feat, "z", n_z)
    tgt_sq, src_sq = squares(tgt), squares(src)
    n_src, n_tgt = src.shape[0] * src.shape[2], n_core * tgt_own
    src_flat = src.transpose(1, 0, 2).reshape(width, n_src)
    tgt_flat = tgt.transpose(1, 0, 2).reshape(width, n_tgt)
    sq_s, sq_t = src_sq.reshape(n_src), tgt_sq.reshape(n_tgt)
    tgt_pot = jnp.zeros((n_tgt,), jnp.float32)

    def blocks(flat):
        return flat.reshape(width, -1, BLOCK).transpose(1, 0, 2)

    for step in range(ITERS):
        part = partial_lse(blocks(tgt_flat), sq_t.reshape(-1, BLOCK), tgt_pot.reshape(-1, BLOCK), src_flat, sq_s)
        src_pot = -EPS * (merge(share(part, "z", n_z)) - math.log(targets))
        part = partial_lse(blocks(src_flat), sq_s.reshape(-1, BLOCK), src_pot.reshape(-1, BLOCK), tgt_flat, sq_t)
        if step < ITERS - 1:
            tgt_pot = -EPS * (merge(share(part, ("row", "core"), n_row * n_core)) - math.log(sources))
        else:
            send = jnp.broadcast_to(part.reshape(1, n_core, tgt_own), (n_row, n_core, tgt_own))
            got = lax.all_to_all(send.reshape(n_row * n_core, tgt_own), ("row", "core"), 0, 0, tiled=True)
            tgt_out = -EPS * (merge(got) - math.log(sources))
    both = lax.all_gather(src_pot.reshape(n_z, -1), "core", axis=1)
    return both.reshape(n_core * n_src), tgt_out


def solution(mesh):
    n_row, n_col = mesh.shape["row"], mesh.shape["col"]
    n_core = 2
    n_z = n_col // n_core
    fine = Mesh(mesh.devices.reshape(n_row, n_z, n_core), ("row", "z", "core"))

    def body(src_feat, tgt_feat):
        return per_device(n_row, n_z, n_core, src_feat, tgt_feat)

    return jax.shard_map(
        body,
        mesh=fine,
        in_specs=(P(None, ("row", "z", "core")), P(None, ("z", "core"))),
        out_specs=(P("row"), P(("z", "core"))),
        check_vma=False,
    )
```

```python
import functools
import math

import jax
import jax.numpy as jnp
from jax import lax
from jax.experimental import pallas as pl
from jax.experimental.pallas import tpu as pltpu
from jax.sharding import Mesh, PartitionSpec as P

ITERS = 2
INV_EPS = 20.0
EPS = 0.05
LANES = 128
INNER_GAIN = 2.0 * INV_EPS * math.log2(math.e)
SQ_GAIN = -INV_EPS * math.log2(math.e)
FROM_LOG2 = EPS * math.log(2.0)
LOW, HIGH = -91.0, 100.0
F32, BF16 = jnp.float32, jnp.bfloat16


def split3(v):
    hi = v.astype(BF16)
    rest = v - hi.astype(F32)
    mid = rest.astype(BF16)
    return hi, mid, (rest - mid.astype(F32)).astype(BF16)


def bias_rows(v, own, width):
    row = lax.broadcasted_iota(jnp.int32, (width, LANES), 0)
    other = 3 - own
    out = jnp.where((row >= other) & (row < other + 3), 1.0, 0.0)
    for k, term in enumerate(split3(v)):
        out = jnp.where(row == own + k, term.astype(F32), out)
    return out


def prep_targets(y_ref, yt_ref):
    cores, width, own = y_ref.shape
    for c in range(cores):
        for k in range(0, own, LANES):
            y = y_ref[c, :, k : k + LANES].astype(F32)
            sq = jnp.sum(y * y, axis=0, keepdims=True)
            rows = pl.ds(c * own + k, LANES)
            yt_ref[rows, : 2 * width] = jnp.concatenate([y, y], axis=0).T.astype(BF16)
            tail = bias_rows(SQ_GAIN * sq, 0, width)
            yt_ref[rows, 2 * width :] = jnp.concatenate([y, tail], axis=0).T.astype(BF16)


def scores(yt_ref, xa_ref, rows, cols):
    return jnp.dot(yt_ref[rows, :], xa_ref[:, cols], preferred_element_type=F32)


def merge(parts):
    peak = jnp.max(parts, axis=0)
    return peak + jnp.log2(jnp.sum(jnp.exp2(parts - peak[None]), axis=0))


def spread_to_rows(v, out_ref):
    for k in range(v.shape[0]):
        out_ref[k * LANES : (k + 1) * LANES, :] = jnp.broadcast_to(v[k : k + 1], (LANES, LANES)).T


def slow_over_targets(yt_ref, xa_ref, pot_ref, out_ref):
    n_tgt = yt_ref.shape[0]
    step = 256

    def one(it, _):
        cols = pl.ds(pl.multiple_of(it * LANES, LANES), LANES)

        def tile(jt):
            rows = pl.ds(pl.multiple_of(jt * step, step), step)
            s = scores(yt_ref, xa_ref, rows, cols)
            return s if pot_ref is None else s + pot_ref[rows, :]

        def peak_step(jt, peak):
            return jnp.maximum(peak, jnp.max(tile(jt), axis=0, keepdims=True))

        peak = lax.fori_loop(0, n_tgt // step, peak_step, jnp.full((1, LANES), -jnp.inf, F32))

        def sum_step(jt, total):
            return total + jnp.sum(jnp.exp2(tile(jt) - peak), axis=0, keepdims=True)

        total = lax.fori_loop(0, n_tgt // step, sum_step, jnp.zeros((1, LANES), F32))
        out_ref[pl.ds(it, 1), :] = peak + jnp.log2(total)
        return 0

    lax.fori_loop(0, out_ref.shape[0], one, 0)


def slow_over_sources(yt_ref, xa_ref, pot_ref, out_ref):
    n_blocks = xa_ref.shape[1] // LANES

    def one(jt, _):
        rows = pl.ds(pl.multiple_of(jt * LANES, LANES), LANES)

        def tile(it):
            cols = pl.ds(pl.multiple_of(it * LANES, LANES), LANES)
            return scores(yt_ref, xa_ref, rows, cols) + pot_ref[pl.ds(it, 1), :]

        def peak_step(it, peak):
            return jnp.maximum(peak, tile(it))

        peak = lax.fori_loop(0, n_blocks, peak_step, jnp.full((LANES, LANES), -jnp.inf, F32))
        peak = jnp.max(peak, axis=1, keepdims=True)

        def sum_step(it, total):
            return total + jnp.exp2(tile(it) - peak)

        total = lax.fori_loop(0, n_blocks, sum_step, jnp.zeros((LANES, LANES), F32))
        value = peak + jnp.log2(jnp.sum(total, axis=1, keepdims=True))
        out_ref[pl.ds(jt, 1), :] = jnp.broadcast_to(value, (LANES, LANES)).T[:1]
        return 0

    lax.fori_loop(0, out_ref.shape[0], one, 0)


def send(value, part_ref):
    copies = part_ref.shape[0]
    part_ref[...] = jnp.broadcast_to(value[None], (copies,) + value.shape)


def first_over_targets(tile, yt_ref, x_ref, e_ref, xa_ref, part_ref, sum_ref):
    n_blocks, width, _ = x_ref.shape
    n_tgt = yt_ref.shape[0]
    for b in range(n_blocks):
        x = x_ref[b].astype(F32)
        sq = jnp.sum(x * x, axis=0, keepdims=True)
        tail = bias_rows(SQ_GAIN * sq, 3, width).astype(BF16)
        xa_ref[:, b * LANES : (b + 1) * LANES] = jnp.concatenate([*split3(INNER_GAIN * x), tail], axis=0)
    wide = 2 * LANES

    def one(it, _):
        cols = pl.ds(pl.multiple_of(it * wide, wide), wide)
        acc = jnp.zeros((8, wide), F32)
        for jt in range(0, n_tgt, tile):
            rows = pl.ds(jt, tile)
            e = jnp.exp2(scores(yt_ref, xa_ref, rows, cols))
            e_ref[rows, cols] = e
            acc = acc + jnp.sum(e.reshape(tile // 8, 8, wide), axis=0)
        total = jnp.sum(acc, axis=0, keepdims=True)
        sum_ref[pl.ds(2 * it, 1), :] = total[:, :LANES]
        sum_ref[pl.ds(2 * it + 1, 1), :] = total[:, LANES:]
        return 0

    lax.fori_loop(0, n_blocks // 2, one, 0)
    totals = sum_ref[...]
    fast = (jnp.min(totals) >= 2.0**LOW) & (jnp.max(totals) <= 2.0**HIGH)

    @pl.when(fast)
    def _():
        send(jnp.log2(totals), part_ref)

    @pl.when(jnp.logical_not(fast))
    def _():
        slow_over_targets(yt_ref, xa_ref, None, sum_ref)
        send(sum_ref[...], part_ref)


def checked(totals, pot):
    top = jnp.max(pot)
    floor = jnp.exp2(jnp.minimum(jnp.maximum(top, 0.0), HIGH) + LOW)
    return (top <= HIGH) & (jnp.min(totals) >= floor)


def over_sources(log_targets, rows_at_once, parts_ref, e_ref, yt_ref, xa_ref, part_ref, pot_ref, sum_ref, acc_ref, yt_buf, xa_buf):
    n_tgt, n_src = e_ref.shape
    n_blocks = n_src // LANES
    pot = log_targets - merge(parts_ref[...])
    pot_ref[...] = pot
    u = jnp.exp2(jnp.minimum(pot, HIGH))

    def one(jt, _):
        rows = pl.ds(pl.multiple_of(jt * rows_at_once, rows_at_once), rows_at_once)
        acc = e_ref[rows, :LANES] * u[:1]
        for b in range(1, n_blocks):
            acc = acc + e_ref[rows, b * LANES : (b + 1) * LANES] * u[b : b + 1]
        acc_ref[rows, :] = acc
        return 0

    lax.fori_loop(0, n_tgt // rows_at_once, one, 0)
    for k in range(n_tgt // LANES):
        block = acc_ref[k * LANES : (k + 1) * LANES, :].T
        sum_ref[k : k + 1, :] = jnp.sum(block, axis=0, keepdims=True)
    totals = sum_ref[...]
    fast = checked(totals, pot)

    def put(value):
        copies, n, _ = part_ref.shape
        for k in range(copies):
            at = (k * n) % value.shape[0]
            part_ref[k] = value[at : at + n]

    @pl.when(fast)
    def _():
        put(jnp.log2(totals))

    @pl.when(jnp.logical_not(fast))
    def _():
        pltpu.sync_copy(yt_ref, yt_buf)
        pltpu.sync_copy(xa_ref, xa_buf)
        slow_over_sources(yt_buf, xa_buf, pot_ref, sum_ref)
        put(sum_ref[...])


def over_targets(log_sources, rows_at_once, parts_ref, e_ref, yt_ref, xa_ref, part_ref, sum_ref, pot_ref, yt_buf, xa_buf):
    n_tgt, n_src = e_ref.shape
    n_blocks = n_src // LANES
    pot = log_sources - merge(parts_ref[...])
    spread_to_rows(jnp.exp2(jnp.minimum(pot, HIGH)), pot_ref)

    def one(jt, acc):
        acc = list(acc)
        for r in range(rows_at_once // 8):
            rows = pl.ds(pl.multiple_of(jt * rows_at_once + 8 * r, 8), 8)
            v = pot_ref[rows, :]
            for b in range(n_blocks):
                acc[b] = acc[b] + e_ref[rows, b * LANES : (b + 1) * LANES] * v
        return tuple(acc)

    acc = lax.fori_loop(0, n_tgt // rows_at_once, one, (jnp.zeros((8, LANES), F32),) * n_blocks)
    for b in range(n_blocks):
        sum_ref[b : b + 1, :] = jnp.sum(acc[b], axis=0, keepdims=True)
    totals = sum_ref[...]
    fast = checked(totals, pot)

    @pl.when(fast)
    def _():
        send(jnp.log2(totals), part_ref)

    @pl.when(jnp.logical_not(fast))
    def _():
        pltpu.sync_copy(yt_ref, yt_buf)
        pltpu.sync_copy(xa_ref, xa_buf)
        spread_to_rows(pot, pot_ref)
        slow_over_targets(yt_buf, xa_buf, pot_ref, sum_ref)
        send(sum_ref[...], part_ref)


VMEM = pl.BlockSpec(memory_space=pltpu.VMEM)
ANY = pl.BlockSpec(memory_space=pl.ANY)
LIMIT = 20 << 20


def params():
    return pltpu.CompilerParams(vmem_limit_bytes=LIMIT)


def call_prep(y):
    cores, width, own = y.shape
    return pl.pallas_call(
        prep_targets,
        out_shape=jax.ShapeDtypeStruct((cores * own, 4 * width), BF16),
        in_specs=[VMEM],
        out_specs=VMEM,
        compiler_params=params(),
        name="prep_targets",
    )(y)


def call_first(yt, x, copies, tile=512):
    n_blocks, width, lanes = x.shape
    n_tgt, n_src = yt.shape[0], n_blocks * lanes
    return pl.pallas_call(
        functools.partial(first_over_targets, tile),
        out_shape=(
            pltpu.VMEM((n_tgt, n_src), F32),
            jax.ShapeDtypeStruct((4 * width, n_src), BF16),
            jax.ShapeDtypeStruct((copies, n_blocks, lanes), F32),
        ),
        in_specs=[VMEM, VMEM],
        out_specs=(VMEM, VMEM, VMEM),
        scratch_shapes=[pltpu.VMEM((n_blocks, lanes), F32)],
        compiler_params=params(),
        name="first_over_targets",
    )(yt, x)


def call_over_sources(log_targets, parts, e, yt, xa, part_shape, rows_at_once=32):
    n_tgt, n_src = e.shape
    return pl.pallas_call(
        functools.partial(over_sources, log_targets, rows_at_once),
        out_shape=(
            jax.ShapeDtypeStruct(part_shape, F32),
            jax.ShapeDtypeStruct((n_src // LANES, LANES), F32),
        ),
        in_specs=[VMEM, VMEM, ANY, ANY],
        out_specs=(VMEM, VMEM),
        scratch_shapes=[
            pltpu.VMEM((n_tgt // LANES, LANES), F32),
            pltpu.VMEM((n_tgt, LANES), F32),
            pltpu.VMEM(yt.shape, BF16),
            pltpu.VMEM(xa.shape, BF16),
        ],
        compiler_params=params(),
        name="over_sources",
    )(parts, e, yt, xa)


def call_over_targets(log_sources, parts, e, yt, xa, copies, rows_at_once=32):
    n_tgt, n_src = e.shape
    return pl.pallas_call(
        functools.partial(over_targets, log_sources, rows_at_once),
        out_shape=jax.ShapeDtypeStruct((copies, n_src // LANES, LANES), F32),
        in_specs=[VMEM, VMEM, ANY, ANY],
        out_specs=VMEM,
        scratch_shapes=[
            pltpu.VMEM((n_src // LANES, LANES), F32),
            pltpu.VMEM((n_tgt, LANES), F32),
            pltpu.VMEM(yt.shape, BF16),
            pltpu.VMEM(xa.shape, BF16),
        ],
        compiler_params=params(),
        name="over_targets",
    )(parts, e, yt, xa)


def exchange(value, axis):
    return lax.all_to_all(value, axis, 0, 0, tiled=False)


def per_device(n_row, n_z, n_core, src_feat, tgt_feat):
    width, src_own = src_feat.shape
    tgt_own = tgt_feat.shape[1]
    log_sources = math.log2(src_own * n_row * n_z * n_core)
    log_targets = math.log2(tgt_own * n_z * n_core)
    n_tgt = n_core * tgt_own
    group = n_row * n_core
    x = exchange(jnp.broadcast_to(src_feat[None], (n_z, width, src_own)), "z")
    yt = call_prep(lax.all_gather(tgt_feat, "core"))
    e, xa, part = call_first(yt, x, n_z)
    for step in range(ITERS):
        parts = exchange(part, "z")
        if step < ITERS - 1:
            part, _ = call_over_sources(log_targets, parts, e, yt, xa, (group, n_tgt // LANES, LANES))
            parts = exchange(part, ("row", "core"))
            part = call_over_targets(log_sources, parts, e, yt, xa, n_z)
        else:
            part, src = call_over_sources(log_targets, parts, e, yt, xa, (group, tgt_own // LANES, LANES))
            parts = exchange(part, ("row", "core"))
    tgt_pot = FROM_LOG2 * (log_sources - merge(parts)).reshape(tgt_own)
    src = lax.all_gather(src, "core", axis=1)
    return FROM_LOG2 * src.reshape(n_core * n_z * src_own), tgt_pot


def solution(mesh):
    n_row, n_col = mesh.shape["row"], mesh.shape["col"]
    n_core = 2
    n_z = n_col // n_core
    fine = Mesh(mesh.devices.reshape(n_row, n_z, n_core), ("row", "z", "core"))
    return jax.shard_map(
        functools.partial(per_device, n_row, n_z, n_core),
        mesh=fine,
        in_specs=(P(None, ("row", "z", "core")), P(None, ("z", "core"))),
        out_specs=(P("row"), P(("z", "core"))),
        check_vma=False,
    )
```

```python
import functools
import math

import jax
import jax.numpy as jnp
from jax import lax
from jax.experimental import pallas as pl
from jax.experimental.pallas import tpu as pltpu
from jax.sharding import Mesh, PartitionSpec as P

ITERS = 2
INV_EPS = 20.0
EPS = 0.05
LANES = 128
INNER_GAIN = 2.0 * INV_EPS * math.log2(math.e)
SQ_GAIN = -INV_EPS * math.log2(math.e)
FROM_LOG2 = EPS * math.log(2.0)
LOW, HIGH = -91.0, 100.0
F32, BF16 = jnp.float32, jnp.bfloat16


def split3(v):
    hi = v.astype(BF16)
    rest = v - hi.astype(F32)
    mid = rest.astype(BF16)
    return hi, mid, (rest - mid.astype(F32)).astype(BF16)


def bias_rows(v, own, width):
    row = lax.broadcasted_iota(jnp.int32, (width, LANES), 0)
    other = 3 - own
    out = jnp.where((row >= other) & (row < other + 3), 1.0, 0.0)
    for k, term in enumerate(split3(v)):
        out = jnp.where(row == own + k, term.astype(F32), out)
    return out


def prep_targets(y_ref, yt_ref):
    cores, width, own = y_ref.shape
    for c in range(cores):
        for k in range(0, own, LANES):
            y = y_ref[c, :, k : k + LANES].astype(F32)
            sq = jnp.sum(y * y, axis=0, keepdims=True)
            rows = pl.ds(c * own + k, LANES)
            yt_ref[rows, : 2 * width] = jnp.concatenate([y, y], axis=0).T.astype(BF16)
            tail = bias_rows(SQ_GAIN * sq, 0, width)
            yt_ref[rows, 2 * width :] = jnp.concatenate([y, tail], axis=0).T.astype(BF16)


def scores(yt_ref, xa_ref, rows, cols):
    return jnp.dot(yt_ref[rows, :], xa_ref[:, cols], preferred_element_type=F32)


def merge(parts):
    peak = jnp.max(parts, axis=0)
    return peak + jnp.log2(jnp.sum(jnp.exp2(parts - peak[None]), axis=0))


def spread_to_rows(v, out_ref):
    for k in range(v.shape[0]):
        out_ref[k * LANES : (k + 1) * LANES, :] = jnp.broadcast_to(v[k : k + 1], (LANES, LANES)).T


def slow_over_targets(yt_ref, xa_ref, pot_ref, out_ref):
    n_tgt = yt_ref.shape[0]
    step = 256

    def one(it, _):
        cols = pl.ds(pl.multiple_of(it * LANES, LANES), LANES)

        def tile(jt):
            rows = pl.ds(pl.multiple_of(jt * step, step), step)
            s = scores(yt_ref, xa_ref, rows, cols)
            return s if pot_ref is None else s + pot_ref[rows, :]

        def peak_step(jt, peak):
            return jnp.maximum(peak, jnp.max(tile(jt), axis=0, keepdims=True))

        peak = lax.fori_loop(0, n_tgt // step, peak_step, jnp.full((1, LANES), -jnp.inf, F32))

        def sum_step(jt, total):
            return total + jnp.sum(jnp.exp2(tile(jt) - peak), axis=0, keepdims=True)

        total = lax.fori_loop(0, n_tgt // step, sum_step, jnp.zeros((1, LANES), F32))
        out_ref[pl.ds(it, 1), :] = peak + jnp.log2(total)
        return 0

    lax.fori_loop(0, out_ref.shape[0], one, 0)


def slow_over_sources(yt_ref, xa_ref, pot_ref, out_ref):
    n_blocks = xa_ref.shape[1] // LANES

    def one(jt, _):
        rows = pl.ds(pl.multiple_of(jt * LANES, LANES), LANES)

        def tile(it):
            cols = pl.ds(pl.multiple_of(it * LANES, LANES), LANES)
            return scores(yt_ref, xa_ref, rows, cols) + pot_ref[pl.ds(it, 1), :]

        def peak_step(it, peak):
            return jnp.maximum(peak, tile(it))

        peak = lax.fori_loop(0, n_blocks, peak_step, jnp.full((LANES, LANES), -jnp.inf, F32))
        peak = jnp.max(peak, axis=1, keepdims=True)

        def sum_step(it, total):
            return total + jnp.exp2(tile(it) - peak)

        total = lax.fori_loop(0, n_blocks, sum_step, jnp.zeros((LANES, LANES), F32))
        value = peak + jnp.log2(jnp.sum(total, axis=1, keepdims=True))
        out_ref[pl.ds(jt, 1), :] = jnp.broadcast_to(value, (LANES, LANES)).T[:1]
        return 0

    lax.fori_loop(0, out_ref.shape[0], one, 0)


def send(value, part_ref):
    copies = part_ref.shape[0]
    part_ref[...] = jnp.broadcast_to(value[None], (copies,) + value.shape)


def first_over_targets(tile, yt_ref, x_ref, e_ref, xa_ref, part_ref, sum_ref):
    n_blocks, width, _ = x_ref.shape
    n_tgt = yt_ref.shape[0]
    n_src = n_blocks * LANES
    for b in range(n_blocks):
        x = x_ref[b].astype(F32)
        sq = jnp.sum(x * x, axis=0, keepdims=True)
        tail = bias_rows(SQ_GAIN * sq, 3, width).astype(BF16)
        xa_ref[:, b * LANES : (b + 1) * LANES] = jnp.concatenate([*split3(INNER_GAIN * x), tail], axis=0)
    acc = jnp.zeros((8, n_src), F32)
    for jt in range(0, n_tgt, tile):
        e = jnp.exp2(scores(yt_ref, xa_ref, pl.ds(jt, tile), slice(None)))
        e_ref[jt : jt + tile, :] = e
        acc = acc + jnp.sum(e.reshape(tile // 8, 8, n_src), axis=0)
    total = jnp.sum(acc, axis=0, keepdims=True)
    for b in range(n_blocks):
        sum_ref[b : b + 1, :] = total[:, b * LANES : (b + 1) * LANES]
    totals = sum_ref[...]
    send(jnp.log2(totals), part_ref)
    fast = (jnp.min(totals) >= 2.0**LOW) & (jnp.max(totals) <= 2.0**HIGH)

    @pl.when(jnp.logical_not(fast))
    def _():
        slow_over_targets(yt_ref, xa_ref, None, sum_ref)
        send(sum_ref[...], part_ref)


def checked(totals, pot):
    top = jnp.max(pot)
    floor = jnp.exp2(jnp.minimum(jnp.maximum(top, 0.0), HIGH) + LOW)
    return (top <= HIGH) & (jnp.min(totals) >= floor)


def over_sources(log_targets, at_once, parts_ref, e_ref, yt_ref, xa_ref, part_ref, sum_ref, pot_ref, acc_ref, yt_buf, xa_buf):
    n_tgt, n_src = e_ref.shape
    n_blocks = n_src // LANES
    pot = log_targets - merge(parts_ref[...])
    pot_ref[...] = pot
    u = jnp.exp2(jnp.minimum(pot, HIGH))
    u = [jnp.broadcast_to(u[b : b + 1], (8, LANES)) for b in range(n_blocks)]

    def one(jt, _):
        for r in range(0, at_once, 8):
            rows = pl.ds(pl.multiple_of(jt * at_once + r, 8), 8)
            acc = e_ref[rows, :LANES] * u[0]
            for b in range(1, n_blocks):
                acc = acc + e_ref[rows, b * LANES : (b + 1) * LANES] * u[b]
            acc_ref[rows, :] = acc
        return 0

    lax.fori_loop(0, n_tgt // at_once, one, 0)
    for k in range(n_tgt // LANES):
        block = acc_ref[k * LANES : (k + 1) * LANES, :].T
        sum_ref[k : k + 1, :] = jnp.sum(block, axis=0, keepdims=True)
    totals = sum_ref[...]

    def put(value):
        copies, n, _ = part_ref.shape
        for k in range(copies):
            at = (k * n) % value.shape[0]
            part_ref[k] = value[at : at + n]

    put(jnp.log2(totals))

    @pl.when(jnp.logical_not(checked(totals, pot)))
    def _():
        pltpu.sync_copy(yt_ref, yt_buf)
        pltpu.sync_copy(xa_ref, xa_buf)
        slow_over_sources(yt_buf, xa_buf, pot_ref, sum_ref)
        put(sum_ref[...])


def over_targets(log_sources, at_once, parts_ref, e_ref, yt_ref, xa_ref, part_ref, sum_ref, pot_ref, yt_buf, xa_buf):
    n_tgt, n_src = e_ref.shape
    n_blocks = n_src // LANES
    pot = log_sources - merge(parts_ref[...])
    spread_to_rows(jnp.exp2(jnp.minimum(pot, HIGH)), pot_ref)

    def one(jt, acc):
        acc = list(acc)
        for r in range(0, at_once, 8):
            rows = pl.ds(pl.multiple_of(jt * at_once + r, 8), 8)
            v = pot_ref[rows, :]
            for b in range(n_blocks):
                acc[b] = acc[b] + e_ref[rows, b * LANES : (b + 1) * LANES] * v
        return tuple(acc)

    acc = lax.fori_loop(0, n_tgt // at_once, one, (jnp.zeros((8, LANES), F32),) * n_blocks)
    for b in range(n_blocks):
        sum_ref[b : b + 1, :] = jnp.sum(acc[b], axis=0, keepdims=True)
    totals = sum_ref[...]
    send(jnp.log2(totals), part_ref)

    @pl.when(jnp.logical_not(checked(totals, pot)))
    def _():
        pltpu.sync_copy(yt_ref, yt_buf)
        pltpu.sync_copy(xa_ref, xa_buf)
        spread_to_rows(pot, pot_ref)
        slow_over_targets(yt_buf, xa_buf, pot_ref, sum_ref)
        send(sum_ref[...], part_ref)


def make_copies(x_ref, out_ref):
    send(x_ref[...], out_ref)


def finish_targets(log_sources, parts_ref, out_ref):
    out_ref[...] = FROM_LOG2 * (log_sources - merge(parts_ref[...]))


VMEM = pl.BlockSpec(memory_space=pltpu.VMEM)
ANY = pl.BlockSpec(memory_space=pl.ANY)
LIMIT = 20 << 20


def params():
    return pltpu.CompilerParams(vmem_limit_bytes=LIMIT)


def call_prep(y):
    cores, width, own = y.shape
    return pl.pallas_call(
        prep_targets,
        out_shape=jax.ShapeDtypeStruct((cores * own, 4 * width), BF16),
        in_specs=[VMEM],
        out_specs=VMEM,
        compiler_params=params(),
        name="prep_targets",
    )(y)


def call_copies(x, copies):
    return pl.pallas_call(
        make_copies,
        out_shape=jax.ShapeDtypeStruct((copies,) + x.shape, x.dtype),
        in_specs=[VMEM],
        out_specs=VMEM,
        compiler_params=params(),
        name="make_copies",
    )(x)


def call_finish(log_sources, parts):
    return pl.pallas_call(
        functools.partial(finish_targets, log_sources),
        out_shape=jax.ShapeDtypeStruct(parts.shape[1:], F32),
        in_specs=[VMEM],
        out_specs=VMEM,
        compiler_params=params(),
        name="finish_targets",
    )(parts)


def call_first(yt, x, copies, tile=128):
    n_blocks, width, lanes = x.shape
    n_tgt, n_src = yt.shape[0], n_blocks * lanes
    return pl.pallas_call(
        functools.partial(first_over_targets, tile),
        out_shape=(
            pltpu.VMEM((n_tgt, n_src), F32),
            jax.ShapeDtypeStruct((4 * width, n_src), BF16),
            jax.ShapeDtypeStruct((copies, n_blocks, lanes), F32),
        ),
        in_specs=[VMEM, VMEM],
        out_specs=(VMEM, VMEM, VMEM),
        scratch_shapes=[pltpu.VMEM((n_blocks, lanes), F32)],
        compiler_params=params(),
        name="first_over_targets",
    )(yt, x)


def call_over_sources(log_targets, parts, e, yt, xa, part_shape, at_once=128):
    n_tgt, n_src = e.shape
    return pl.pallas_call(
        functools.partial(over_sources, log_targets, at_once),
        out_shape=jax.ShapeDtypeStruct(part_shape, F32),
        in_specs=[VMEM, VMEM, ANY, ANY],
        out_specs=VMEM,
        scratch_shapes=[
            pltpu.VMEM((n_tgt // LANES, LANES), F32),
            pltpu.VMEM((n_src // LANES, LANES), F32),
            pltpu.VMEM((n_tgt, LANES), F32),
            pltpu.VMEM(yt.shape, BF16),
            pltpu.VMEM(xa.shape, BF16),
        ],
        compiler_params=params(),
        name="over_sources",
    )(parts, e, yt, xa)


def call_over_targets(log_sources, parts, e, yt, xa, copies, at_once=128):
    n_tgt, n_src = e.shape
    return pl.pallas_call(
        functools.partial(over_targets, log_sources, at_once),
        out_shape=jax.ShapeDtypeStruct((copies, n_src // LANES, LANES), F32),
        in_specs=[VMEM, VMEM, ANY, ANY],
        out_specs=VMEM,
        scratch_shapes=[
            pltpu.VMEM((n_src // LANES, LANES), F32),
            pltpu.VMEM((n_tgt, LANES), F32),
            pltpu.VMEM(yt.shape, BF16),
            pltpu.VMEM(xa.shape, BF16),
        ],
        compiler_params=params(),
        name="over_targets",
    )(parts, e, yt, xa)


def exchange(value, axis):
    return lax.all_to_all(value, axis, 0, 0, tiled=False)


def per_device(n_row, n_z, n_core, src_feat, tgt_feat):
    width, src_own = src_feat.shape
    tgt_own = tgt_feat.shape[1]
    log_sources = math.log2(src_own * n_row * n_z * n_core)
    log_targets = math.log2(tgt_own * n_z * n_core)
    n_tgt = n_core * tgt_own
    group = n_row * n_core
    x = exchange(call_copies(src_feat, n_z), "z")
    yt = call_prep(lax.all_gather(tgt_feat, "core"))
    e, xa, part = call_first(yt, x, n_z)
    for step in range(ITERS):
        parts = exchange(part, "z")
        if step < ITERS - 1:
            part = call_over_sources(log_targets, parts, e, yt, xa, (group, n_tgt // LANES, LANES))
            part = call_over_targets(log_sources, exchange(part, ("row", "core")), e, yt, xa, n_z)
        else:
            part = call_over_sources(log_targets, parts, e, yt, xa, (group, tgt_own // LANES, LANES))
            src_pot = FROM_LOG2 * (log_targets - merge(parts))
            src_pot = lax.all_gather(src_pot, "core", axis=1)
            tgt_pot = call_finish(log_sources, exchange(part, ("row", "core")))
    return src_pot.reshape(n_core * n_z * src_own), tgt_pot.reshape(tgt_own)


def solution(mesh):
    n_row, n_col = mesh.shape["row"], mesh.shape["col"]
    n_core = 2
    n_z = n_col // n_core
    fine = Mesh(mesh.devices.reshape(n_row, n_z, n_core), ("row", "z", "core"))
    return jax.shard_map(
        functools.partial(per_device, n_row, n_z, n_core),
        mesh=fine,
        in_specs=(P(None, ("row", "z", "core")), P(None, ("z", "core"))),
        out_specs=(P("row"), P(("z", "core"))),
        check_vma=False,
    )
```

```python
import functools
import math

import jax
import jax.numpy as jnp
from jax import lax
from jax.experimental import pallas as pl
from jax.experimental.pallas import tpu as pltpu
from jax.sharding import Mesh, PartitionSpec as P

INV_EPS = 20.0
EPS = 0.05
LANES = 128
INNER_GAIN = 2.0 * INV_EPS * math.log2(math.e)
SQ_GAIN = -INV_EPS * math.log2(math.e)
FROM_LOG2 = EPS * math.log(2.0)
LOW, HIGH = -91.0, 100.0
F32, BF16 = jnp.float32, jnp.bfloat16


def split3(v):
    hi = v.astype(BF16)
    rest = v - hi.astype(F32)
    mid = rest.astype(BF16)
    return hi, mid, (rest - mid.astype(F32)).astype(BF16)


def bias_rows(v, own, width):
    row = lax.broadcasted_iota(jnp.int32, (width, LANES), 0)
    other = 3 - own
    out = jnp.where((row >= other) & (row < other + 3), 1.0, 0.0)
    for k, term in enumerate(split3(v)):
        out = jnp.where(row == own + k, term.astype(F32), out)
    return out


def prep_targets(y_ref, yt_ref):
    cores, width, own = y_ref.shape
    for c in range(cores):
        for k in range(0, own, LANES):
            y = y_ref[c, :, k : k + LANES].astype(F32)
            sq = jnp.sum(y * y, axis=0, keepdims=True)
            rows = pl.ds(c * own + k, LANES)
            yt_ref[rows, : 2 * width] = jnp.concatenate([y, y], axis=0).T.astype(BF16)
            tail = bias_rows(SQ_GAIN * sq, 0, width)
            yt_ref[rows, 2 * width :] = jnp.concatenate([y, tail], axis=0).T.astype(BF16)


def scores(yt_ref, xa_ref, rows, cols):
    return jnp.dot(yt_ref[rows, :], xa_ref[:, cols], preferred_element_type=F32)


def merge(parts):
    peak = jnp.max(parts, axis=0)
    return peak + jnp.log2(jnp.sum(jnp.exp2(parts - peak[None]), axis=0))


def spread_to_rows(v, out_ref):
    for k in range(v.shape[0]):
        out_ref[k * LANES : (k + 1) * LANES, :] = jnp.broadcast_to(v[k : k + 1], (LANES, LANES)).T


def slow_over_targets(yt_ref, xa_ref, pot_ref, out_ref):
    n_tgt = yt_ref.shape[0]
    step = 256

    def one(it, _):
        cols = pl.ds(pl.multiple_of(it * LANES, LANES), LANES)

        def tile(jt):
            rows = pl.ds(pl.multiple_of(jt * step, step), step)
            s = scores(yt_ref, xa_ref, rows, cols)
            return s if pot_ref is None else s + pot_ref[rows, :]

        def peak_step(jt, peak):
            return jnp.maximum(peak, jnp.max(tile(jt), axis=0, keepdims=True))

        peak = lax.fori_loop(0, n_tgt // step, peak_step, jnp.full((1, LANES), -jnp.inf, F32))

        def sum_step(jt, total):
            return total + jnp.sum(jnp.exp2(tile(jt) - peak), axis=0, keepdims=True)

        total = lax.fori_loop(0, n_tgt // step, sum_step, jnp.zeros((1, LANES), F32))
        out_ref[pl.ds(it, 1), :] = peak + jnp.log2(total)
        return 0

    lax.fori_loop(0, out_ref.shape[0], one, 0)


def slow_over_sources(yt_ref, xa_ref, pot_ref, out_ref):
    n_blocks = xa_ref.shape[1] // LANES

    def one(jt, _):
        rows = pl.ds(pl.multiple_of(jt * LANES, LANES), LANES)

        def tile(it):
            cols = pl.ds(pl.multiple_of(it * LANES, LANES), LANES)
            return scores(yt_ref, xa_ref, rows, cols) + pot_ref[pl.ds(it, 1), :]

        def peak_step(it, peak):
            return jnp.maximum(peak, tile(it))

        peak = lax.fori_loop(0, n_blocks, peak_step, jnp.full((LANES, LANES), -jnp.inf, F32))
        peak = jnp.max(peak, axis=1, keepdims=True)

        def sum_step(it, total):
            return total + jnp.exp2(tile(it) - peak)

        total = lax.fori_loop(0, n_blocks, sum_step, jnp.zeros((LANES, LANES), F32))
        value = peak + jnp.log2(jnp.sum(total, axis=1, keepdims=True))
        out_ref[pl.ds(jt, 1), :] = jnp.broadcast_to(value, (LANES, LANES)).T[:1]
        return 0

    lax.fori_loop(0, out_ref.shape[0], one, 0)


def send(value, part_ref):
    copies = part_ref.shape[0]
    part_ref[...] = jnp.broadcast_to(value[None], (copies,) + value.shape)


def first_over_targets(tile, yt_ref, x_ref, e_ref, xa_ref, part_ref, sum_ref):
    n_blocks, width, _ = x_ref.shape
    n_tgt = yt_ref.shape[0]
    n_src = n_blocks * LANES
    for b in range(n_blocks):
        x = x_ref[b].astype(F32)
        sq = jnp.sum(x * x, axis=0, keepdims=True)
        tail = bias_rows(SQ_GAIN * sq, 3, width).astype(BF16)
        xa_ref[:, b * LANES : (b + 1) * LANES] = jnp.concatenate([*split3(INNER_GAIN * x), tail], axis=0)
    acc = jnp.zeros((8, n_src), F32)
    for jt in range(0, n_tgt, tile):
        e = jnp.exp2(scores(yt_ref, xa_ref, pl.ds(jt, tile), slice(None)))
        e_ref[jt : jt + tile, :] = e
        acc = acc + jnp.sum(e.reshape(tile // 8, 8, n_src), axis=0)
    total = jnp.sum(acc, axis=0, keepdims=True)
    for b in range(n_blocks):
        sum_ref[b : b + 1, :] = total[:, b * LANES : (b + 1) * LANES]
    totals = sum_ref[...]
    send(jnp.log2(totals), part_ref)
    fast = (jnp.min(totals) >= 2.0**LOW) & (jnp.max(totals) <= 2.0**HIGH)

    @pl.when(jnp.logical_not(fast))
    def _():
        slow_over_targets(yt_ref, xa_ref, None, sum_ref)
        send(sum_ref[...], part_ref)


def checked(totals, pot):
    top = jnp.max(pot)
    floor = jnp.exp2(jnp.minimum(jnp.maximum(top, 0.0), HIGH) + LOW)
    return (top <= HIGH) & (jnp.min(totals) >= floor)


def changed(before, change):
    return before + change.astype(F32)


def over_sources(log_targets, at_once, n_parts, *refs):
    parts_refs, refs = refs[:n_parts], refs[n_parts:]
    e_ref, yt_ref, xa_ref, part_ref, sum_ref, pot_ref, acc_ref, yt_buf, xa_buf = refs
    n_tgt, n_src = e_ref.shape
    n_blocks = n_src // LANES
    parts = [ref[...] for ref in parts_refs]
    pot = log_targets - merge(parts[0] if n_parts == 1 else changed(*parts))
    pot_ref[...] = pot
    u = jnp.exp2(jnp.minimum(pot, HIGH))
    u = [jnp.broadcast_to(u[b : b + 1], (8, LANES)) for b in range(n_blocks)]

    def one(jt, _):
        for r in range(0, at_once, 8):
            rows = pl.ds(pl.multiple_of(jt * at_once + r, 8), 8)
            acc = e_ref[rows, :LANES] * u[0]
            for b in range(1, n_blocks):
                acc = acc + e_ref[rows, b * LANES : (b + 1) * LANES] * u[b]
            acc_ref[rows, :] = acc
        return 0

    lax.fori_loop(0, n_tgt // at_once, one, 0)
    for k in range(n_tgt // LANES):
        block = acc_ref[k * LANES : (k + 1) * LANES, :].T
        sum_ref[k : k + 1, :] = jnp.sum(block, axis=0, keepdims=True)
    totals = sum_ref[...]

    def put(value):
        copies, n, _ = part_ref.shape
        for k in range(copies):
            at = (k * n) % value.shape[0]
            part_ref[k] = value[at : at + n]

    put(jnp.log2(totals))

    @pl.when(jnp.logical_not(checked(totals, pot)))
    def _():
        pltpu.sync_copy(yt_ref, yt_buf)
        pltpu.sync_copy(xa_ref, xa_buf)
        slow_over_sources(yt_buf, xa_buf, pot_ref, sum_ref)
        put(sum_ref[...])


def over_targets(log_sources, at_once, parts_ref, before_ref, e_ref, yt_ref, xa_ref, part_ref, sum_ref, pot_ref, yt_buf, xa_buf):
    n_tgt, n_src = e_ref.shape
    n_blocks = n_src // LANES
    pot = log_sources - merge(parts_ref[...])
    spread_to_rows(jnp.exp2(jnp.minimum(pot, HIGH)), pot_ref)

    def one(jt, acc):
        acc = list(acc)
        for r in range(0, at_once, 8):
            rows = pl.ds(pl.multiple_of(jt * at_once + r, 8), 8)
            v = pot_ref[rows, :]
            for b in range(n_blocks):
                acc[b] = acc[b] + e_ref[rows, b * LANES : (b + 1) * LANES] * v
        return tuple(acc)

    acc = lax.fori_loop(0, n_tgt // at_once, one, (jnp.zeros((8, LANES), F32),) * n_blocks)
    for b in range(n_blocks):
        sum_ref[b : b + 1, :] = jnp.sum(acc[b], axis=0, keepdims=True)
    totals = sum_ref[...]
    before = before_ref[0]
    send((jnp.log2(totals) - before).astype(BF16), part_ref)

    @pl.when(jnp.logical_not(checked(totals, pot)))
    def _():
        pltpu.sync_copy(yt_ref, yt_buf)
        pltpu.sync_copy(xa_ref, xa_buf)
        spread_to_rows(pot, pot_ref)
        slow_over_targets(yt_buf, xa_buf, pot_ref, sum_ref)
        send((sum_ref[...] - before).astype(BF16), part_ref)


def make_copies(x_ref, out_ref, sems):
    copies = [pltpu.make_async_copy(x_ref, out_ref.at[k], sems.at[k]) for k in range(out_ref.shape[0])]
    for copy in copies:
        copy.start()
    for copy in copies:
        copy.wait()


def finish_targets(log_sources, parts_ref, out_ref):
    out_ref[...] = FROM_LOG2 * (log_sources - merge(parts_ref[...]))


VMEM = pl.BlockSpec(memory_space=pltpu.VMEM)
ANY = pl.BlockSpec(memory_space=pl.ANY)
LIMIT = 20 << 20


def params():
    return pltpu.CompilerParams(vmem_limit_bytes=LIMIT)


def call_prep(y):
    cores, width, own = y.shape
    return pl.pallas_call(
        prep_targets,
        out_shape=jax.ShapeDtypeStruct((cores * own, 4 * width), BF16),
        in_specs=[VMEM],
        out_specs=VMEM,
        compiler_params=params(),
        name="prep_targets",
    )(y)


def call_copies(x, copies):
    return pl.pallas_call(
        make_copies,
        out_shape=pltpu.HBM((copies,) + x.shape, x.dtype),
        in_specs=[ANY],
        out_specs=ANY,
        scratch_shapes=[pltpu.SemaphoreType.DMA((copies,))],
        compiler_params=params(),
        name="make_copies",
    )(pltpu.with_memory_space_constraint(x, pltpu.HBM))


def call_finish(log_sources, parts):
    return pl.pallas_call(
        functools.partial(finish_targets, log_sources),
        out_shape=jax.ShapeDtypeStruct(parts.shape[1:], F32),
        in_specs=[VMEM],
        out_specs=VMEM,
        compiler_params=params(),
        name="finish_targets",
    )(parts)


def call_first(yt, x, copies, tile=128):
    n_blocks, width, lanes = x.shape
    n_tgt, n_src = yt.shape[0], n_blocks * lanes
    return pl.pallas_call(
        functools.partial(first_over_targets, tile),
        out_shape=(
            pltpu.VMEM((n_tgt, n_src), F32),
            jax.ShapeDtypeStruct((4 * width, n_src), BF16),
            jax.ShapeDtypeStruct((copies, n_blocks, lanes), F32),
        ),
        in_specs=[VMEM, VMEM],
        out_specs=(VMEM, VMEM, VMEM),
        scratch_shapes=[pltpu.VMEM((n_blocks, lanes), F32)],
        compiler_params=params(),
        name="first_over_targets",
    )(yt, x)


def call_over_sources(log_targets, e, yt, xa, part_shape, *parts, at_once=128):
    n_tgt, n_src = e.shape
    return pl.pallas_call(
        functools.partial(over_sources, log_targets, at_once, len(parts)),
        out_shape=jax.ShapeDtypeStruct(part_shape, F32),
        in_specs=[VMEM] * len(parts) + [VMEM, ANY, ANY],
        out_specs=VMEM,
        scratch_shapes=[
            pltpu.VMEM((n_tgt // LANES, LANES), F32),
            pltpu.VMEM((n_src // LANES, LANES), F32),
            pltpu.VMEM((n_tgt, LANES), F32),
            pltpu.VMEM(yt.shape, BF16),
            pltpu.VMEM(xa.shape, BF16),
        ],
        compiler_params=params(),
        name="over_sources",
    )(*parts, e, yt, xa)


def call_over_targets(log_sources, parts, before, e, yt, xa, copies, at_once=128):
    n_tgt, n_src = e.shape
    return pl.pallas_call(
        functools.partial(over_targets, log_sources, at_once),
        out_shape=jax.ShapeDtypeStruct((copies, n_src // LANES, LANES), BF16),
        in_specs=[VMEM, VMEM, VMEM, ANY, ANY],
        out_specs=VMEM,
        scratch_shapes=[
            pltpu.VMEM((n_src // LANES, LANES), F32),
            pltpu.VMEM((n_tgt, LANES), F32),
            pltpu.VMEM(yt.shape, BF16),
            pltpu.VMEM(xa.shape, BF16),
        ],
        compiler_params=params(),
        name="over_targets",
    )(parts, before, e, yt, xa)


def exchange(value, axis):
    return lax.all_to_all(value, axis, 0, 0, tiled=False)


def per_device(n_row, n_z, n_core, src_feat, tgt_feat):
    width, src_own = src_feat.shape
    tgt_own = tgt_feat.shape[1]
    log_sources = math.log2(src_own * n_row * n_z * n_core)
    log_targets = math.log2(tgt_own * n_z * n_core)
    n_tgt = n_core * tgt_own
    group = n_row * n_core
    x = exchange(call_copies(src_feat, n_z), "z")
    yt = call_prep(lax.all_gather(tgt_feat, "core"))
    e, xa, part = call_first(yt, x, n_z)
    first = exchange(part, "z")
    col_part = call_over_sources(log_targets, e, yt, xa, (group, n_tgt // LANES, LANES), first)
    col_parts = exchange(col_part, ("row", "core"))
    change = exchange(call_over_targets(log_sources, col_parts, part, e, yt, xa, n_z), "z")
    col_part = call_over_sources(log_targets, e, yt, xa, (group, tgt_own // LANES, LANES), first, change)
    src_pot = FROM_LOG2 * (log_targets - merge(changed(first, change)))
    src_pot = lax.all_gather(src_pot, "core", axis=1)
    tgt_pot = call_finish(log_sources, exchange(col_part, ("row", "core")))
    return src_pot.reshape(n_core * n_z * src_own), tgt_pot.reshape(tgt_own)


def solution(mesh):
    n_row, n_col = mesh.shape["row"], mesh.shape["col"]
    n_core = 2
    n_z = n_col // n_core
    fine = Mesh(mesh.devices.reshape(n_row, n_z, n_core), ("row", "z", "core"))
    return jax.shard_map(
        functools.partial(per_device, n_row, n_z, n_core),
        mesh=fine,
        in_specs=(P(None, ("row", "z", "core")), P(None, ("z", "core"))),
        out_specs=(P("row"), P(("z", "core"))),
        check_vma=False,
    )
```

```python
import functools
import math

import jax
import jax.numpy as jnp
from jax import lax
from jax.experimental import pallas as pl
from jax.experimental.pallas import tpu as pltpu
from jax.sharding import Mesh, PartitionSpec as P

INV_EPS = 20.0
EPS = 0.05
LANES = 128
INNER_GAIN = 2.0 * INV_EPS * math.log2(math.e)
SQ_GAIN = -INV_EPS * math.log2(math.e)
FROM_LOG2 = EPS * math.log(2.0)
LOW, HIGH = -91.0, 100.0
F32, BF16 = jnp.float32, jnp.bfloat16
POWER, SHIFT, SMALL = 11.0, -22.0, 2.0**-9


def split3(v):
    hi = v.astype(BF16)
    rest = v - hi.astype(F32)
    mid = rest.astype(BF16)
    return hi, mid, (rest - mid.astype(F32)).astype(BF16)


def bias_rows(v, own, width):
    row = lax.broadcasted_iota(jnp.int32, (width, LANES), 0)
    other = 3 - own
    out = jnp.where((row >= other) & (row < other + 3), 1.0, 0.0)
    for k, term in enumerate(split3(v)):
        out = jnp.where(row == own + k, term.astype(F32), out)
    return out


def prep_targets(y_ref, yt_ref):
    cores, width, own = y_ref.shape
    for c in range(cores):
        for k in range(0, own, LANES):
            y = y_ref[c, :, k : k + LANES].astype(F32)
            sq = jnp.sum(y * y, axis=0, keepdims=True)
            rows = pl.ds(c * own + k, LANES)
            yt_ref[rows, : 2 * width] = jnp.concatenate([y, y], axis=0).T.astype(BF16)
            tail = bias_rows(SQ_GAIN * sq, 0, width)
            yt_ref[rows, 2 * width :] = jnp.concatenate([y, tail], axis=0).T.astype(BF16)


def scores(yt_ref, xa_ref, rows, cols):
    return jnp.dot(yt_ref[rows, :], xa_ref[:, cols], preferred_element_type=F32)


def merge(parts):
    peak = jnp.max(parts, axis=0)
    return peak + jnp.log2(jnp.sum(jnp.exp2(parts - peak[None]), axis=0))


def encode(d):
    size = jnp.abs(d)
    t = jnp.exp2(POWER * jnp.log2(jnp.maximum(size, SMALL)) + SHIFT)
    t = jnp.where(size < SMALL, 0.0, t)
    return jnp.where(d < 0.0, -t, t).astype(BF16)


def decode(code):
    t = code.astype(F32)
    size = jnp.abs(t)
    d = jnp.exp2((jnp.log2(jnp.maximum(size, 2.0**-126)) - SHIFT) * (1.0 / POWER))
    d = jnp.where(size > 0.0, d, 0.0)
    return jnp.where(t < 0.0, -d, d)


def spread_to_rows(v, out_ref):
    for k in range(v.shape[0]):
        out_ref[k * LANES : (k + 1) * LANES, :] = jnp.broadcast_to(v[k : k + 1], (LANES, LANES)).T


def slow_over_targets(yt_ref, xa_ref, pot_ref, out_ref):
    n_tgt = yt_ref.shape[0]
    step = 256

    def one(it, _):
        cols = pl.ds(pl.multiple_of(it * LANES, LANES), LANES)

        def tile(jt):
            rows = pl.ds(pl.multiple_of(jt * step, step), step)
            s = scores(yt_ref, xa_ref, rows, cols)
            return s if pot_ref is None else s + pot_ref[rows, :]

        def peak_step(jt, peak):
            return jnp.maximum(peak, jnp.max(tile(jt), axis=0, keepdims=True))

        peak = lax.fori_loop(0, n_tgt // step, peak_step, jnp.full((1, LANES), -jnp.inf, F32))

        def sum_step(jt, total):
            return total + jnp.sum(jnp.exp2(tile(jt) - peak), axis=0, keepdims=True)

        total = lax.fori_loop(0, n_tgt // step, sum_step, jnp.zeros((1, LANES), F32))
        out_ref[pl.ds(it, 1), :] = peak + jnp.log2(total)
        return 0

    lax.fori_loop(0, out_ref.shape[0], one, 0)


def slow_over_sources(yt_ref, xa_ref, pot_ref, out_ref):
    n_blocks = xa_ref.shape[1] // LANES

    def one(jt, _):
        rows = pl.ds(pl.multiple_of(jt * LANES, LANES), LANES)

        def tile(it):
            cols = pl.ds(pl.multiple_of(it * LANES, LANES), LANES)
            return scores(yt_ref, xa_ref, rows, cols) + pot_ref[pl.ds(it, 1), :]

        def peak_step(it, peak):
            return jnp.maximum(peak, tile(it))

        peak = lax.fori_loop(0, n_blocks, peak_step, jnp.full((LANES, LANES), -jnp.inf, F32))
        peak = jnp.max(peak, axis=1, keepdims=True)

        def sum_step(it, total):
            return total + jnp.exp2(tile(it) - peak)

        total = lax.fori_loop(0, n_blocks, sum_step, jnp.zeros((LANES, LANES), F32))
        value = peak + jnp.log2(jnp.sum(total, axis=1, keepdims=True))
        out_ref[pl.ds(jt, 1), :] = jnp.broadcast_to(value, (LANES, LANES)).T[:1]
        return 0

    lax.fori_loop(0, out_ref.shape[0], one, 0)


def send(value, part_ref):
    copies = part_ref.shape[0]
    part_ref[...] = jnp.broadcast_to(value[None], (copies,) + value.shape)


def first_over_targets(tile, yt_ref, x_ref, e_ref, xa_ref, part_ref, sum_ref):
    n_blocks, width, _ = x_ref.shape
    n_tgt = yt_ref.shape[0]
    n_src = n_blocks * LANES
    for b in range(n_blocks):
        x = x_ref[b].astype(F32)
        sq = jnp.sum(x * x, axis=0, keepdims=True)
        tail = bias_rows(SQ_GAIN * sq, 3, width).astype(BF16)
        xa_ref[:, b * LANES : (b + 1) * LANES] = jnp.concatenate([*split3(INNER_GAIN * x), tail], axis=0)
    acc = jnp.zeros((8, n_src), F32)
    for jt in range(0, n_tgt, tile):
        e = jnp.exp2(scores(yt_ref, xa_ref, pl.ds(jt, tile), slice(None)))
        e_ref[jt : jt + tile, :] = e
        acc = acc + jnp.sum(e.reshape(tile // 8, 8, n_src), axis=0)
    total = jnp.sum(acc, axis=0, keepdims=True)
    for b in range(n_blocks):
        sum_ref[b : b + 1, :] = total[:, b * LANES : (b + 1) * LANES]
    totals = sum_ref[...]
    send(jnp.log2(totals), part_ref)
    fast = (jnp.min(totals) >= 2.0**LOW) & (jnp.max(totals) <= 2.0**HIGH)

    @pl.when(jnp.logical_not(fast))
    def _():
        slow_over_targets(yt_ref, xa_ref, None, sum_ref)
        send(sum_ref[...], part_ref)


def checked(totals, pot):
    top = jnp.max(pot)
    floor = jnp.exp2(jnp.minimum(jnp.maximum(top, 0.0), HIGH) + LOW)
    return (top <= HIGH) & (jnp.min(totals) >= floor)


def row_sums(first, *codes):
    return first + sum(decode(code) for code in codes)


def over_sources(log_targets, at_once, n_parts, *refs):
    parts_refs, refs = refs[:n_parts], refs[n_parts:]
    e_ref, yt_ref, xa_ref, part_ref, sum_ref, pot_ref, acc_ref, yt_buf, xa_buf = refs
    n_tgt, n_src = e_ref.shape
    n_blocks = n_src // LANES
    pot = log_targets - merge(row_sums(*[ref[...] for ref in parts_refs]))
    pot_ref[...] = pot
    u = jnp.exp2(jnp.minimum(pot, HIGH))
    u = [jnp.broadcast_to(u[b : b + 1], (8, LANES)) for b in range(n_blocks)]

    def one(jt, _):
        for r in range(0, at_once, 8):
            rows = pl.ds(pl.multiple_of(jt * at_once + r, 8), 8)
            acc = e_ref[rows, :LANES] * u[0]
            for b in range(1, n_blocks):
                acc = acc + e_ref[rows, b * LANES : (b + 1) * LANES] * u[b]
            acc_ref[rows, :] = acc
        return 0

    lax.fori_loop(0, n_tgt // at_once, one, 0)
    for k in range(n_tgt // LANES):
        block = acc_ref[k * LANES : (k + 1) * LANES, :].T
        sum_ref[k : k + 1, :] = jnp.sum(block, axis=0, keepdims=True)
    totals = sum_ref[...]

    def put(value):
        copies, n, _ = part_ref.shape
        if part_ref.dtype == BF16:
            value = encode(value - math.log2(n_src))
        for k in range(copies):
            at = (k * n) % value.shape[0]
            part_ref[k] = value[at : at + n]

    put(jnp.log2(totals))

    @pl.when(jnp.logical_not(checked(totals, pot)))
    def _():
        pltpu.sync_copy(yt_ref, yt_buf)
        pltpu.sync_copy(xa_ref, xa_buf)
        slow_over_sources(yt_buf, xa_buf, pot_ref, sum_ref)
        put(sum_ref[...])


def over_targets(log_sources, at_once, parts_ref, before_ref, e_ref, yt_ref, xa_ref, part_ref, sum_ref, pot_ref, yt_buf, xa_buf):
    n_tgt, n_src = e_ref.shape
    n_blocks = n_src // LANES
    pot = log_sources - merge(math.log2(n_src) + decode(parts_ref[...]))
    spread_to_rows(jnp.exp2(jnp.minimum(pot, HIGH)), pot_ref)

    def one(jt, acc):
        acc = list(acc)
        for r in range(0, at_once, 8):
            rows = pl.ds(pl.multiple_of(jt * at_once + r, 8), 8)
            v = pot_ref[rows, :]
            for b in range(n_blocks):
                acc[b] = acc[b] + e_ref[rows, b * LANES : (b + 1) * LANES] * v
        return tuple(acc)

    acc = lax.fori_loop(0, n_tgt // at_once, one, (jnp.zeros((8, LANES), F32),) * n_blocks)
    for b in range(n_blocks):
        sum_ref[b : b + 1, :] = jnp.sum(acc[b], axis=0, keepdims=True)
    totals = sum_ref[...]
    before = before_ref[0]
    send(encode(jnp.log2(totals) - before), part_ref)

    @pl.when(jnp.logical_not(checked(totals, pot)))
    def _():
        pltpu.sync_copy(yt_ref, yt_buf)
        pltpu.sync_copy(xa_ref, xa_buf)
        spread_to_rows(pot, pot_ref)
        slow_over_targets(yt_buf, xa_buf, pot_ref, sum_ref)
        send(encode(sum_ref[...] - before), part_ref)


def make_copies(x_ref, out_ref):
    send(x_ref[...], out_ref)


def finish_targets(log_sources, parts_ref, out_ref):
    out_ref[...] = FROM_LOG2 * (log_sources - merge(parts_ref[...]))


VMEM = pl.BlockSpec(memory_space=pltpu.VMEM)
ANY = pl.BlockSpec(memory_space=pl.ANY)
LIMIT = 20 << 20


def params():
    return pltpu.CompilerParams(vmem_limit_bytes=LIMIT)


def call_prep(y):
    cores, width, own = y.shape
    return pl.pallas_call(
        prep_targets,
        out_shape=jax.ShapeDtypeStruct((cores * own, 4 * width), BF16),
        in_specs=[VMEM],
        out_specs=VMEM,
        compiler_params=params(),
        name="prep_targets",
    )(y)


def call_copies(x, copies):
    return pl.pallas_call(
        make_copies,
        out_shape=jax.ShapeDtypeStruct((copies,) + x.shape, x.dtype),
        in_specs=[VMEM],
        out_specs=VMEM,
        compiler_params=params(),
        name="make_copies",
    )(x)


def call_finish(log_sources, parts):
    return pl.pallas_call(
        functools.partial(finish_targets, log_sources),
        out_shape=jax.ShapeDtypeStruct(parts.shape[1:], F32),
        in_specs=[VMEM],
        out_specs=VMEM,
        compiler_params=params(),
        name="finish_targets",
    )(parts)


def call_first(yt, x, copies, tile=128):
    n_blocks, width, lanes = x.shape
    n_tgt, n_src = yt.shape[0], n_blocks * lanes
    return pl.pallas_call(
        functools.partial(first_over_targets, tile),
        out_shape=(
            pltpu.VMEM((n_tgt, n_src), F32),
            jax.ShapeDtypeStruct((4 * width, n_src), BF16),
            jax.ShapeDtypeStruct((copies, n_blocks, lanes), F32),
        ),
        in_specs=[VMEM, VMEM],
        out_specs=(VMEM, VMEM, VMEM),
        scratch_shapes=[pltpu.VMEM((n_blocks, lanes), F32)],
        compiler_params=params(),
        name="first_over_targets",
    )(yt, x)


def call_over_sources(log_targets, e, yt, xa, part_shape, part_type, *parts, at_once=128):
    n_tgt, n_src = e.shape
    return pl.pallas_call(
        functools.partial(over_sources, log_targets, at_once, len(parts)),
        out_shape=jax.ShapeDtypeStruct(part_shape, part_type),
        in_specs=[VMEM] * len(parts) + [VMEM, ANY, ANY],
        out_specs=VMEM,
        scratch_shapes=[
            pltpu.VMEM((n_tgt // LANES, LANES), F32),
            pltpu.VMEM((n_src // LANES, LANES), F32),
            pltpu.VMEM((n_tgt, LANES), F32),
            pltpu.VMEM(yt.shape, BF16),
            pltpu.VMEM(xa.shape, BF16),
        ],
        compiler_params=params(),
        name="over_sources",
    )(*parts, e, yt, xa)


def call_over_targets(log_sources, parts, before, e, yt, xa, copies, at_once=128):
    n_tgt, n_src = e.shape
    return pl.pallas_call(
        functools.partial(over_targets, log_sources, at_once),
        out_shape=jax.ShapeDtypeStruct((copies, n_src // LANES, LANES), BF16),
        in_specs=[VMEM, VMEM, VMEM, ANY, ANY],
        out_specs=VMEM,
        scratch_shapes=[
            pltpu.VMEM((n_src // LANES, LANES), F32),
            pltpu.VMEM((n_tgt, LANES), F32),
            pltpu.VMEM(yt.shape, BF16),
            pltpu.VMEM(xa.shape, BF16),
        ],
        compiler_params=params(),
        name="over_targets",
    )(parts, before, e, yt, xa)


def exchange(value, axis):
    return lax.all_to_all(value, axis, 0, 0, tiled=False)


def per_device(n_row, n_z, n_core, src_feat, tgt_feat):
    width, src_own = src_feat.shape
    tgt_own = tgt_feat.shape[1]
    log_sources = math.log2(src_own * n_row * n_z * n_core)
    log_targets = math.log2(tgt_own * n_z * n_core)
    n_tgt = n_core * tgt_own
    group = n_row * n_core
    x = exchange(call_copies(src_feat, n_z), "z")
    yt = call_prep(lax.all_gather(tgt_feat, "core"))
    e, xa, part = call_first(yt, x, n_z)
    first = exchange(part, "z")
    col_part = call_over_sources(log_targets, e, yt, xa, (group, n_tgt // LANES, LANES), BF16, first)
    col_parts = exchange(col_part, ("row", "core"))
    change = exchange(call_over_targets(log_sources, col_parts, part, e, yt, xa, n_z), "z")
    col_part = call_over_sources(log_targets, e, yt, xa, (group, tgt_own // LANES, LANES), F32, first, change)
    src_pot = FROM_LOG2 * (log_targets - merge(row_sums(first, change)))
    src_pot = lax.all_gather(src_pot, "core", axis=1)
    tgt_pot = call_finish(log_sources, exchange(col_part, ("row", "core")))
    return src_pot.reshape(n_core * n_z * src_own), tgt_pot.reshape(tgt_own)


def solution(mesh):
    n_row, n_col = mesh.shape["row"], mesh.shape["col"]
    n_core = 2
    n_z = n_col // n_core
    fine = Mesh(mesh.devices.reshape(n_row, n_z, n_core), ("row", "z", "core"))
    return jax.shard_map(
        functools.partial(per_device, n_row, n_z, n_core),
        mesh=fine,
        in_specs=(P(None, ("row", "z", "core")), P(None, ("z", "core"))),
        out_specs=(P("row"), P(("z", "core"))),
        check_vma=False,
    )
```

```python
import functools
import math

import jax
import jax.numpy as jnp
from jax import lax
from jax.experimental import pallas as pl
from jax.experimental.pallas import tpu as pltpu
from jax.sharding import Mesh, PartitionSpec as P

INV_EPS = 20.0
EPS = 0.05
LANES = 128
INNER_GAIN = 2.0 * INV_EPS * math.log2(math.e)
SQ_GAIN = -INV_EPS * math.log2(math.e)
FROM_LOG2 = EPS * math.log(2.0)
LOW, HIGH = -91.0, 100.0
F32, BF16 = jnp.float32, jnp.bfloat16
ABOVE, BELOW, SHIFT, SMALL = 14.0, 4.0, -57.0, 2.0**-17


def split3(v):
    hi = v.astype(BF16)
    rest = v - hi.astype(F32)
    mid = rest.astype(BF16)
    return hi, mid, (rest - mid.astype(F32)).astype(BF16)


def bias_rows(v, own, width):
    row = lax.broadcasted_iota(jnp.int32, (width, LANES), 0)
    other = 3 - own
    out = jnp.where((row >= other) & (row < other + 3), 1.0, 0.0)
    for k, term in enumerate(split3(v)):
        out = jnp.where(row == own + k, term.astype(F32), out)
    return out


def prep_targets(y_ref, yt_ref):
    cores, width, own = y_ref.shape
    for c in range(cores):
        for k in range(0, own, LANES):
            y = y_ref[c, :, k : k + LANES].astype(F32)
            sq = jnp.sum(y * y, axis=0, keepdims=True)
            rows = pl.ds(c * own + k, LANES)
            yt_ref[rows, : 2 * width] = jnp.concatenate([y, y], axis=0).T.astype(BF16)
            tail = bias_rows(SQ_GAIN * sq, 0, width)
            yt_ref[rows, 2 * width :] = jnp.concatenate([y, tail], axis=0).T.astype(BF16)


def scores(yt_ref, xa_ref, rows, cols):
    return jnp.dot(yt_ref[rows, :], xa_ref[:, cols], preferred_element_type=F32)


def merge(parts):
    peak = jnp.max(parts, axis=0)
    return peak + jnp.log2(jnp.sum(jnp.exp2(parts - peak[None]), axis=0))


def encode(d):
    size = jnp.abs(d)
    log = jnp.log2(jnp.maximum(size, SMALL))
    t = jnp.exp2(log * jnp.where(log > 0.0, ABOVE, BELOW) + SHIFT)
    t = jnp.where(size < SMALL, 0.0, t)
    return jnp.where(d < 0.0, -t, t).astype(BF16)


def decode(code):
    t = code.astype(F32)
    size = jnp.abs(t)
    log = jnp.log2(jnp.maximum(size, 2.0**-126)) - SHIFT
    d = jnp.exp2(log * jnp.where(log > 0.0, 1.0 / ABOVE, 1.0 / BELOW))
    d = jnp.where(size > 0.0, d, 0.0)
    return jnp.where(t < 0.0, -d, d)


def base_of(d, around):
    a, b, c = (d[..., :1, k : k + 1] + around for k in range(3))
    base = jnp.maximum(jnp.minimum(a, b), jnp.minimum(jnp.maximum(a, b), c))
    at = [lax.broadcasted_iota(jnp.int32, d.shape, d.ndim - k) for k in (2, 1)]
    return base, (at[0] == 0) & (at[1] < 3)


def encode_from_base(value, around):
    head = encode(value - around)
    base, first = base_of(decode(head), around)
    return jnp.where(first, head.astype(F32), encode(value - base).astype(F32)).astype(BF16)


def decode_from_base(code, around):
    d = decode(code)
    base, first = base_of(d, around)
    return jnp.where(first, around, base) + d


def spread_to_rows(v, out_ref):
    for k in range(v.shape[0]):
        out_ref[k * LANES : (k + 1) * LANES, :] = jnp.broadcast_to(v[k : k + 1], (LANES, LANES)).T


def slow_over_targets(yt_ref, xa_ref, pot_ref, out_ref):
    n_tgt = yt_ref.shape[0]
    step = 256

    def one(it, _):
        cols = pl.ds(pl.multiple_of(it * LANES, LANES), LANES)

        def tile(jt):
            rows = pl.ds(pl.multiple_of(jt * step, step), step)
            s = scores(yt_ref, xa_ref, rows, cols)
            return s if pot_ref is None else s + pot_ref[rows, :]

        def peak_step(jt, peak):
            return jnp.maximum(peak, jnp.max(tile(jt), axis=0, keepdims=True))

        peak = lax.fori_loop(0, n_tgt // step, peak_step, jnp.full((1, LANES), -jnp.inf, F32))

        def sum_step(jt, total):
            return total + jnp.sum(jnp.exp2(tile(jt) - peak), axis=0, keepdims=True)

        total = lax.fori_loop(0, n_tgt // step, sum_step, jnp.zeros((1, LANES), F32))
        out_ref[pl.ds(it, 1), :] = peak + jnp.log2(total)
        return 0

    lax.fori_loop(0, out_ref.shape[0], one, 0)


def slow_over_sources(yt_ref, xa_ref, pot_ref, out_ref):
    n_blocks = xa_ref.shape[1] // LANES

    def one(jt, _):
        rows = pl.ds(pl.multiple_of(jt * LANES, LANES), LANES)

        def tile(it):
            cols = pl.ds(pl.multiple_of(it * LANES, LANES), LANES)
            return scores(yt_ref, xa_ref, rows, cols) + pot_ref[pl.ds(it, 1), :]

        def peak_step(it, peak):
            return jnp.maximum(peak, tile(it))

        peak = lax.fori_loop(0, n_blocks, peak_step, jnp.full((LANES, LANES), -jnp.inf, F32))
        peak = jnp.max(peak, axis=1, keepdims=True)

        def sum_step(it, total):
            return total + jnp.exp2(tile(it) - peak)

        total = lax.fori_loop(0, n_blocks, sum_step, jnp.zeros((LANES, LANES), F32))
        value = peak + jnp.log2(jnp.sum(total, axis=1, keepdims=True))
        out_ref[pl.ds(jt, 1), :] = jnp.broadcast_to(value, (LANES, LANES)).T[:1]
        return 0

    lax.fori_loop(0, out_ref.shape[0], one, 0)


def send(value, part_ref):
    copies = part_ref.shape[0]
    part_ref[...] = jnp.broadcast_to(value[None], (copies,) + value.shape)


def first_over_targets(tile, yt_ref, x_ref, e_ref, xa_ref, part_ref, sum_ref):
    n_blocks, width, _ = x_ref.shape
    n_tgt = yt_ref.shape[0]
    n_src = n_blocks * LANES
    for b in range(n_blocks):
        x = x_ref[b].astype(F32)
        sq = jnp.sum(x * x, axis=0, keepdims=True)
        tail = bias_rows(SQ_GAIN * sq, 3, width).astype(BF16)
        xa_ref[:, b * LANES : (b + 1) * LANES] = jnp.concatenate([*split3(INNER_GAIN * x), tail], axis=0)
    acc = jnp.zeros((8, n_src), F32)
    for jt in range(0, n_tgt, tile):
        e = jnp.exp2(scores(yt_ref, xa_ref, pl.ds(jt, tile), slice(None)))
        e_ref[jt : jt + tile, :] = e
        acc = acc + jnp.sum(e.reshape(tile // 8, 8, n_src), axis=0)
    total = jnp.sum(acc, axis=0, keepdims=True)
    for b in range(n_blocks):
        sum_ref[b : b + 1, :] = total[:, b * LANES : (b + 1) * LANES]
    totals = sum_ref[...]
    send(encode_from_base(jnp.log2(totals), math.log2(n_tgt)), part_ref)
    fast = (jnp.min(totals) >= 2.0**LOW) & (jnp.max(totals) <= 2.0**HIGH)

    @pl.when(jnp.logical_not(fast))
    def _():
        slow_over_targets(yt_ref, xa_ref, None, sum_ref)
        send(encode_from_base(sum_ref[...], math.log2(n_tgt)), part_ref)


def checked(totals, pot):
    top = jnp.max(pot)
    floor = jnp.exp2(jnp.minimum(jnp.maximum(top, 0.0), HIGH) + LOW)
    return (top <= HIGH) & (jnp.min(totals) >= floor)


def row_sums(n_tgt, first, *changes):
    return decode_from_base(first, math.log2(n_tgt)) + sum(decode(change) for change in changes)


def over_sources(log_targets, at_once, n_parts, *refs):
    parts_refs, refs = refs[:n_parts], refs[n_parts:]
    e_ref, yt_ref, xa_ref, part_ref, sum_ref, pot_ref, acc_ref, yt_buf, xa_buf = refs
    n_tgt, n_src = e_ref.shape
    n_blocks = n_src // LANES
    pot = log_targets - merge(row_sums(n_tgt, *[ref[...] for ref in parts_refs]))
    pot_ref[...] = pot
    u = jnp.exp2(jnp.minimum(pot, HIGH))
    u = [jnp.broadcast_to(u[b : b + 1], (8, LANES)) for b in range(n_blocks)]

    def one(jt, _):
        for r in range(0, at_once, 8):
            rows = pl.ds(pl.multiple_of(jt * at_once + r, 8), 8)
            acc = e_ref[rows, :LANES] * u[0]
            for b in range(1, n_blocks):
                acc = acc + e_ref[rows, b * LANES : (b + 1) * LANES] * u[b]
            acc_ref[rows, :] = acc
        return 0

    lax.fori_loop(0, n_tgt // at_once, one, 0)
    for k in range(n_tgt // LANES):
        block = acc_ref[k * LANES : (k + 1) * LANES, :].T
        sum_ref[k : k + 1, :] = jnp.sum(block, axis=0, keepdims=True)
    totals = sum_ref[...]

    def put(value):
        copies, n, _ = part_ref.shape
        if part_ref.dtype == BF16:
            value = encode(value - math.log2(n_src))
        for k in range(copies):
            at = (k * n) % value.shape[0]
            part_ref[k] = value[at : at + n]

    put(jnp.log2(totals))

    @pl.when(jnp.logical_not(checked(totals, pot)))
    def _():
        pltpu.sync_copy(yt_ref, yt_buf)
        pltpu.sync_copy(xa_ref, xa_buf)
        slow_over_sources(yt_buf, xa_buf, pot_ref, sum_ref)
        put(sum_ref[...])


def over_targets(log_sources, at_once, parts_ref, before_ref, e_ref, yt_ref, xa_ref, part_ref, sum_ref, pot_ref, yt_buf, xa_buf):
    n_tgt, n_src = e_ref.shape
    n_blocks = n_src // LANES
    pot = log_sources - merge(math.log2(n_src) + decode(parts_ref[...]))
    spread_to_rows(jnp.exp2(jnp.minimum(pot, HIGH)), pot_ref)

    def one(jt, acc):
        acc = list(acc)
        for r in range(0, at_once, 8):
            rows = pl.ds(pl.multiple_of(jt * at_once + r, 8), 8)
            v = pot_ref[rows, :]
            for b in range(n_blocks):
                acc[b] = acc[b] + e_ref[rows, b * LANES : (b + 1) * LANES] * v
        return tuple(acc)

    acc = lax.fori_loop(0, n_tgt // at_once, one, (jnp.zeros((8, LANES), F32),) * n_blocks)
    for b in range(n_blocks):
        sum_ref[b : b + 1, :] = jnp.sum(acc[b], axis=0, keepdims=True)
    totals = sum_ref[...]
    before = row_sums(n_tgt, before_ref[0])
    send(encode(jnp.log2(totals) - before), part_ref)

    @pl.when(jnp.logical_not(checked(totals, pot)))
    def _():
        pltpu.sync_copy(yt_ref, yt_buf)
        pltpu.sync_copy(xa_ref, xa_buf)
        spread_to_rows(pot, pot_ref)
        slow_over_targets(yt_buf, xa_buf, pot_ref, sum_ref)
        send(encode(sum_ref[...] - before), part_ref)


def make_copies(x_ref, out_ref):
    send(x_ref[...], out_ref)


def finish_targets(log_sources, parts_ref, out_ref):
    out_ref[...] = FROM_LOG2 * (log_sources - merge(parts_ref[...]))


VMEM = pl.BlockSpec(memory_space=pltpu.VMEM)
ANY = pl.BlockSpec(memory_space=pl.ANY)
LIMIT = 20 << 20


def params():
    return pltpu.CompilerParams(vmem_limit_bytes=LIMIT)


def call_prep(y):
    cores, width, own = y.shape
    return pl.pallas_call(
        prep_targets,
        out_shape=jax.ShapeDtypeStruct((cores * own, 4 * width), BF16),
        in_specs=[VMEM],
        out_specs=VMEM,
        compiler_params=params(),
        name="prep_targets",
    )(y)


def call_copies(x, copies):
    return pl.pallas_call(
        make_copies,
        out_shape=jax.ShapeDtypeStruct((copies,) + x.shape, x.dtype),
        in_specs=[VMEM],
        out_specs=VMEM,
        compiler_params=params(),
        name="make_copies",
    )(x)


def call_finish(log_sources, parts):
    return pl.pallas_call(
        functools.partial(finish_targets, log_sources),
        out_shape=jax.ShapeDtypeStruct(parts.shape[1:], F32),
        in_specs=[VMEM],
        out_specs=VMEM,
        compiler_params=params(),
        name="finish_targets",
    )(parts)


def call_first(yt, x, copies, tile=128):
    n_blocks, width, lanes = x.shape
    n_tgt, n_src = yt.shape[0], n_blocks * lanes
    return pl.pallas_call(
        functools.partial(first_over_targets, tile),
        out_shape=(
            pltpu.VMEM((n_tgt, n_src), F32),
            jax.ShapeDtypeStruct((4 * width, n_src), BF16),
            jax.ShapeDtypeStruct((copies, n_blocks, lanes), BF16),
        ),
        in_specs=[VMEM, VMEM],
        out_specs=(VMEM, VMEM, VMEM),
        scratch_shapes=[pltpu.VMEM((n_blocks, lanes), F32)],
        compiler_params=params(),
        name="first_over_targets",
    )(yt, x)


def call_over_sources(log_targets, e, yt, xa, part_shape, part_type, *parts, at_once=128):
    n_tgt, n_src = e.shape
    return pl.pallas_call(
        functools.partial(over_sources, log_targets, at_once, len(parts)),
        out_shape=jax.ShapeDtypeStruct(part_shape, part_type),
        in_specs=[VMEM] * len(parts) + [VMEM, ANY, ANY],
        out_specs=VMEM,
        scratch_shapes=[
            pltpu.VMEM((n_tgt // LANES, LANES), F32),
            pltpu.VMEM((n_src // LANES, LANES), F32),
            pltpu.VMEM((n_tgt, LANES), F32),
            pltpu.VMEM(yt.shape, BF16),
            pltpu.VMEM(xa.shape, BF16),
        ],
        compiler_params=params(),
        name="over_sources",
    )(*parts, e, yt, xa)


def call_over_targets(log_sources, parts, before, e, yt, xa, copies, at_once=128):
    n_tgt, n_src = e.shape
    return pl.pallas_call(
        functools.partial(over_targets, log_sources, at_once),
        out_shape=jax.ShapeDtypeStruct((copies, n_src // LANES, LANES), BF16),
        in_specs=[VMEM, VMEM, VMEM, ANY, ANY],
        out_specs=VMEM,
        scratch_shapes=[
            pltpu.VMEM((n_src // LANES, LANES), F32),
            pltpu.VMEM((n_tgt, LANES), F32),
            pltpu.VMEM(yt.shape, BF16),
            pltpu.VMEM(xa.shape, BF16),
        ],
        compiler_params=params(),
        name="over_targets",
    )(parts, before, e, yt, xa)


def exchange(value, axis):
    return lax.all_to_all(value, axis, 0, 0, tiled=False)


def per_device(n_row, n_z, n_core, src_feat, tgt_feat):
    width, src_own = src_feat.shape
    tgt_own = tgt_feat.shape[1]
    log_sources = math.log2(src_own * n_row * n_z * n_core)
    log_targets = math.log2(tgt_own * n_z * n_core)
    n_tgt = n_core * tgt_own
    group = n_row * n_core
    x = exchange(call_copies(src_feat, n_z), "z")
    yt = call_prep(lax.all_gather(tgt_feat, "core"))
    e, xa, part = call_first(yt, x, n_z)
    first = exchange(part, "z")
    col_part = call_over_sources(log_targets, e, yt, xa, (group, n_tgt // LANES, LANES), BF16, first)
    col_parts = exchange(col_part, ("row", "core"))
    change = exchange(call_over_targets(log_sources, col_parts, part, e, yt, xa, n_z), "z")
    col_part = call_over_sources(log_targets, e, yt, xa, (group, tgt_own // LANES, LANES), F32, first, change)
    src_pot = FROM_LOG2 * (log_targets - merge(row_sums(n_tgt, first, change)))
    src_pot = lax.all_gather(src_pot, "core", axis=1)
    tgt_pot = call_finish(log_sources, exchange(col_part, ("row", "core")))
    return src_pot.reshape(n_core * n_z * src_own), tgt_pot.reshape(tgt_own)


def solution(mesh):
    n_row, n_col = mesh.shape["row"], mesh.shape["col"]
    n_core = 2
    n_z = n_col // n_core
    fine = Mesh(mesh.devices.reshape(n_row, n_z, n_core), ("row", "z", "core"))
    return jax.shard_map(
        functools.partial(per_device, n_row, n_z, n_core),
        mesh=fine,
        in_specs=(P(None, ("row", "z", "core")), P(None, ("z", "core"))),
        out_specs=(P("row"), P(("z", "core"))),
        check_vma=False,
    )
```

```python
import functools
import math

import jax
import jax.numpy as jnp
from jax import lax
from jax.experimental import pallas as pl
from jax.experimental.pallas import tpu as pltpu
from jax.sharding import Mesh, PartitionSpec as P

INV_EPS = 20.0
EPS = 0.05
LANES = 128
INNER_GAIN = 2.0 * INV_EPS * math.log2(math.e)
SQ_GAIN = -INV_EPS * math.log2(math.e)
FROM_LOG2 = EPS * math.log(2.0)
LOW, HIGH = -91.0, 100.0
F32, BF16 = jnp.float32, jnp.bfloat16
ABOVE, BELOW, SHIFT, SMALL = 14.0, 4.0, -57.0, 2.0**-17


def split3(v):
    hi = v.astype(BF16)
    rest = v - hi.astype(F32)
    mid = rest.astype(BF16)
    return hi, mid, (rest - mid.astype(F32)).astype(BF16)


def bias_rows(v, own, width):
    row = lax.broadcasted_iota(jnp.int32, (width, LANES), 0)
    other = 3 - own
    out = jnp.where((row >= other) & (row < other + 3), 1.0, 0.0)
    for k, term in enumerate(split3(v)):
        out = jnp.where(row == own + k, term.astype(F32), out)
    return out


def prep_targets(y_ref, yt_ref):
    cores, width, own = y_ref.shape
    for c in range(cores):
        for k in range(0, own, LANES):
            y = y_ref[c, :, k : k + LANES].astype(F32)
            sq = jnp.sum(y * y, axis=0, keepdims=True)
            rows = pl.ds(c * own + k, LANES)
            yt_ref[rows, : 2 * width] = jnp.concatenate([y, y], axis=0).T.astype(BF16)
            tail = bias_rows(SQ_GAIN * sq, 0, width)
            yt_ref[rows, 2 * width :] = jnp.concatenate([y, tail], axis=0).T.astype(BF16)


def scores(yt_ref, xa_ref, rows, cols):
    return jnp.dot(yt_ref[rows, :], xa_ref[:, cols], preferred_element_type=F32)


def merge(parts):
    peak = jnp.max(parts, axis=0)
    return peak + jnp.log2(jnp.sum(jnp.exp2(parts - peak[None]), axis=0))


def encode(d):
    size = jnp.abs(d)
    log = jnp.log2(jnp.maximum(size, SMALL))
    t = jnp.exp2(log * jnp.where(log > 0.0, ABOVE, BELOW) + SHIFT)
    t = jnp.where(size < SMALL, 0.0, t)
    return jnp.where(d < 0.0, -t, t).astype(BF16)


def decode(code):
    t = code.astype(F32)
    size = jnp.abs(t)
    log = jnp.log2(jnp.maximum(size, 2.0**-126)) - SHIFT
    d = jnp.exp2(log * jnp.where(log > 0.0, 1.0 / ABOVE, 1.0 / BELOW))
    d = jnp.where(size > 0.0, d, 0.0)
    return jnp.where(t < 0.0, -d, d)


def base_of(d, around):
    a, b, c = (d[..., :1, k : k + 1] + around for k in range(3))
    base = jnp.maximum(jnp.minimum(a, b), jnp.minimum(jnp.maximum(a, b), c))
    at = [lax.broadcasted_iota(jnp.int32, d.shape, d.ndim - k) for k in (2, 1)]
    return base, (at[0] == 0) & (at[1] < 3)


def encode_from_base(value, around):
    head = encode(value - around)
    base, first = base_of(decode(head), around)
    return jnp.where(first, head.astype(F32), encode(value - base).astype(F32)).astype(BF16)


def decode_from_base(code, around):
    d = decode(code)
    base, first = base_of(d, around)
    return jnp.where(first, around, base) + d


def spread_to_rows(v, out_ref):
    for k in range(v.shape[0]):
        out_ref[k * LANES : (k + 1) * LANES, :] = jnp.broadcast_to(v[k : k + 1], (LANES, LANES)).T


def slow_over_targets(yt_ref, xa_ref, pot_ref, out_ref):
    n_tgt = yt_ref.shape[0]
    step = 256

    def one(it, _):
        cols = pl.ds(pl.multiple_of(it * LANES, LANES), LANES)

        def tile(jt):
            rows = pl.ds(pl.multiple_of(jt * step, step), step)
            s = scores(yt_ref, xa_ref, rows, cols)
            return s if pot_ref is None else s + pot_ref[rows, :]

        def peak_step(jt, peak):
            return jnp.maximum(peak, jnp.max(tile(jt), axis=0, keepdims=True))

        peak = lax.fori_loop(0, n_tgt // step, peak_step, jnp.full((1, LANES), -jnp.inf, F32))

        def sum_step(jt, total):
            return total + jnp.sum(jnp.exp2(tile(jt) - peak), axis=0, keepdims=True)

        total = lax.fori_loop(0, n_tgt // step, sum_step, jnp.zeros((1, LANES), F32))
        out_ref[pl.ds(it, 1), :] = peak + jnp.log2(total)
        return 0

    lax.fori_loop(0, out_ref.shape[0], one, 0)


def slow_over_sources(yt_ref, xa_ref, pot_ref, out_ref):
    n_blocks = xa_ref.shape[1] // LANES

    def one(jt, _):
        rows = pl.ds(pl.multiple_of(jt * LANES, LANES), LANES)

        def tile(it):
            cols = pl.ds(pl.multiple_of(it * LANES, LANES), LANES)
            return scores(yt_ref, xa_ref, rows, cols) + pot_ref[pl.ds(it, 1), :]

        def peak_step(it, peak):
            return jnp.maximum(peak, tile(it))

        peak = lax.fori_loop(0, n_blocks, peak_step, jnp.full((LANES, LANES), -jnp.inf, F32))
        peak = jnp.max(peak, axis=1, keepdims=True)

        def sum_step(it, total):
            return total + jnp.exp2(tile(it) - peak)

        total = lax.fori_loop(0, n_blocks, sum_step, jnp.zeros((LANES, LANES), F32))
        value = peak + jnp.log2(jnp.sum(total, axis=1, keepdims=True))
        out_ref[pl.ds(jt, 1), :] = jnp.broadcast_to(value, (LANES, LANES)).T[:1]
        return 0

    lax.fori_loop(0, out_ref.shape[0], one, 0)


def send(value, part_ref):
    copies = part_ref.shape[0]
    part_ref[...] = jnp.broadcast_to(value[None], (copies,) + value.shape)


def first_over_targets(tile, yt_ref, x_ref, e_ref, xa_ref, part_ref, sum_ref):
    n_blocks, width, _ = x_ref.shape
    n_tgt = yt_ref.shape[0]
    n_src = n_blocks * LANES
    for b in range(n_blocks):
        x = x_ref[b].astype(F32)
        sq = jnp.sum(x * x, axis=0, keepdims=True)
        tail = bias_rows(SQ_GAIN * sq, 3, width).astype(BF16)
        xa_ref[:, b * LANES : (b + 1) * LANES] = jnp.concatenate([*split3(INNER_GAIN * x), tail], axis=0)
    acc = jnp.zeros((8, n_src), F32)
    for jt in range(0, n_tgt, tile):
        e = jnp.exp2(scores(yt_ref, xa_ref, pl.ds(jt, tile), slice(None)))
        e_ref[jt : jt + tile, :] = e
        acc = acc + jnp.sum(e.reshape(tile // 8, 8, n_src), axis=0)
    total = jnp.sum(acc, axis=0, keepdims=True)
    for b in range(n_blocks):
        sum_ref[b : b + 1, :] = total[:, b * LANES : (b + 1) * LANES]
    totals = sum_ref[...]
    send(encode_from_base(jnp.log2(totals), math.log2(n_tgt)), part_ref)
    fast = (jnp.min(totals) >= 2.0**LOW) & (jnp.max(totals) <= 2.0**HIGH)

    @pl.when(jnp.logical_not(fast))
    def _():
        slow_over_targets(yt_ref, xa_ref, None, sum_ref)
        send(encode_from_base(sum_ref[...], math.log2(n_tgt)), part_ref)


def checked(totals, pot):
    top = jnp.max(pot)
    floor = jnp.exp2(jnp.minimum(jnp.maximum(top, 0.0), HIGH) + LOW)
    return (top <= HIGH) & (jnp.min(totals) >= floor)


def row_sums(n_tgt, first, *changes):
    return decode_from_base(first, math.log2(n_tgt)) + sum(decode(change) for change in changes)


def over_sources(log_targets, at_once, n_parts, *refs):
    parts_refs, refs = refs[:n_parts], refs[n_parts:]
    e_ref, yt_ref, xa_ref, part_ref, sum_ref, pot_ref, acc_ref, yt_buf, xa_buf = refs
    n_tgt, n_src = e_ref.shape
    n_blocks = n_src // LANES
    pot = log_targets - merge(row_sums(n_tgt, *[ref[...] for ref in parts_refs]))
    pot_ref[...] = pot
    u = jnp.exp2(jnp.minimum(pot, HIGH))
    u = [jnp.broadcast_to(u[b : b + 1], (8, LANES)) for b in range(n_blocks)]

    def one(jt, _):
        for r in range(0, at_once, 8):
            rows = pl.ds(pl.multiple_of(jt * at_once + r, 8), 8)
            acc = e_ref[rows, :LANES] * u[0]
            for b in range(1, n_blocks):
                acc = acc + e_ref[rows, b * LANES : (b + 1) * LANES] * u[b]
            acc_ref[rows, :] = acc
        return 0

    lax.fori_loop(0, n_tgt // at_once, one, 0)
    for k in range(n_tgt // LANES):
        block = acc_ref[k * LANES : (k + 1) * LANES, :].T
        sum_ref[k : k + 1, :] = jnp.sum(block, axis=0, keepdims=True)
    totals = sum_ref[...]

    def put(value):
        copies, n, _ = part_ref.shape
        if part_ref.dtype == BF16:
            value = encode(value - math.log2(n_src))
        for k in range(copies):
            at = (k * n) % value.shape[0]
            part_ref[k] = value[at : at + n]

    put(jnp.log2(totals))

    @pl.when(jnp.logical_not(checked(totals, pot)))
    def _():
        pltpu.sync_copy(yt_ref, yt_buf)
        pltpu.sync_copy(xa_ref, xa_buf)
        slow_over_sources(yt_buf, xa_buf, pot_ref, sum_ref)
        put(sum_ref[...])


def over_targets(log_sources, at_once, parts_ref, before_ref, e_ref, yt_ref, xa_ref, part_ref, sum_ref, pot_ref, yt_buf, xa_buf):
    n_tgt, n_src = e_ref.shape
    n_blocks = n_src // LANES
    pot = log_sources - merge(math.log2(n_src) + decode(parts_ref[...]))
    spread_to_rows(jnp.exp2(jnp.minimum(pot, HIGH)), pot_ref)

    def one(jt, acc):
        acc = list(acc)
        for r in range(0, at_once, 8):
            rows = pl.ds(pl.multiple_of(jt * at_once + r, 8), 8)
            v = pot_ref[rows, :]
            for b in range(n_blocks):
                acc[b] = acc[b] + e_ref[rows, b * LANES : (b + 1) * LANES] * v
        return tuple(acc)

    acc = lax.fori_loop(0, n_tgt // at_once, one, (jnp.zeros((8, LANES), F32),) * n_blocks)
    for b in range(n_blocks):
        sum_ref[b : b + 1, :] = jnp.sum(acc[b], axis=0, keepdims=True)
    totals = sum_ref[...]
    before = row_sums(n_tgt, before_ref[0])
    send(encode(jnp.log2(totals) - before), part_ref)

    @pl.when(jnp.logical_not(checked(totals, pot)))
    def _():
        pltpu.sync_copy(yt_ref, yt_buf)
        pltpu.sync_copy(xa_ref, xa_buf)
        spread_to_rows(pot, pot_ref)
        slow_over_targets(yt_buf, xa_buf, pot_ref, sum_ref)
        send(encode(sum_ref[...] - before), part_ref)


def make_copies(x_ref, out_ref):
    send(x_ref[...], out_ref)


def finish_sources(log_targets, n_tgt, first_ref, change_ref, out_ref):
    out_ref[...] = FROM_LOG2 * (log_targets - merge(row_sums(n_tgt, first_ref[...], change_ref[...])))


def finish_targets(log_sources, parts_ref, out_ref):
    out_ref[...] = FROM_LOG2 * (log_sources - merge(parts_ref[...]))


VMEM = pl.BlockSpec(memory_space=pltpu.VMEM)
ANY = pl.BlockSpec(memory_space=pl.ANY)
LIMIT = 20 << 20


def params():
    return pltpu.CompilerParams(vmem_limit_bytes=LIMIT)


def call_prep(y):
    cores, width, own = y.shape
    return pl.pallas_call(
        prep_targets,
        out_shape=jax.ShapeDtypeStruct((cores * own, 4 * width), BF16),
        in_specs=[VMEM],
        out_specs=VMEM,
        compiler_params=params(),
        name="prep_targets",
    )(y)


def call_copies(x, copies):
    return pl.pallas_call(
        make_copies,
        out_shape=jax.ShapeDtypeStruct((copies,) + x.shape, x.dtype),
        in_specs=[VMEM],
        out_specs=VMEM,
        compiler_params=params(),
        name="make_copies",
    )(x)


def call_finish_sources(log_targets, n_tgt, first, change):
    return pl.pallas_call(
        functools.partial(finish_sources, log_targets, n_tgt),
        out_shape=jax.ShapeDtypeStruct(first.shape[1:], F32),
        in_specs=[VMEM, VMEM],
        out_specs=VMEM,
        compiler_params=params(),
        name="finish_sources",
    )(first, change)


def call_finish(log_sources, parts):
    return pl.pallas_call(
        functools.partial(finish_targets, log_sources),
        out_shape=jax.ShapeDtypeStruct(parts.shape[1:], F32),
        in_specs=[VMEM],
        out_specs=VMEM,
        compiler_params=params(),
        name="finish_targets",
    )(parts)


def call_first(yt, x, copies, tile=128):
    n_blocks, width, lanes = x.shape
    n_tgt, n_src = yt.shape[0], n_blocks * lanes
    return pl.pallas_call(
        functools.partial(first_over_targets, tile),
        out_shape=(
            pltpu.VMEM((n_tgt, n_src), F32),
            jax.ShapeDtypeStruct((4 * width, n_src), BF16),
            jax.ShapeDtypeStruct((copies, n_blocks, lanes), BF16),
        ),
        in_specs=[VMEM, VMEM],
        out_specs=(VMEM, VMEM, VMEM),
        scratch_shapes=[pltpu.VMEM((n_blocks, lanes), F32)],
        compiler_params=params(),
        name="first_over_targets",
    )(yt, x)


def call_over_sources(log_targets, e, yt, xa, part_shape, part_type, *parts, at_once=128):
    n_tgt, n_src = e.shape
    return pl.pallas_call(
        functools.partial(over_sources, log_targets, at_once, len(parts)),
        out_shape=jax.ShapeDtypeStruct(part_shape, part_type),
        in_specs=[VMEM] * len(parts) + [VMEM, ANY, ANY],
        out_specs=VMEM,
        scratch_shapes=[
            pltpu.VMEM((n_tgt // LANES, LANES), F32),
            pltpu.VMEM((n_src // LANES, LANES), F32),
            pltpu.VMEM((n_tgt, LANES), F32),
            pltpu.VMEM(yt.shape, BF16),
            pltpu.VMEM(xa.shape, BF16),
        ],
        compiler_params=params(),
        name="over_sources",
    )(*parts, e, yt, xa)


def call_over_targets(log_sources, parts, before, e, yt, xa, copies, at_once=128):
    n_tgt, n_src = e.shape
    return pl.pallas_call(
        functools.partial(over_targets, log_sources, at_once),
        out_shape=jax.ShapeDtypeStruct((copies, n_src // LANES, LANES), BF16),
        in_specs=[VMEM, VMEM, VMEM, ANY, ANY],
        out_specs=VMEM,
        scratch_shapes=[
            pltpu.VMEM((n_src // LANES, LANES), F32),
            pltpu.VMEM((n_tgt, LANES), F32),
            pltpu.VMEM(yt.shape, BF16),
            pltpu.VMEM(xa.shape, BF16),
        ],
        compiler_params=params(),
        name="over_targets",
    )(parts, before, e, yt, xa)


def exchange(value, axis):
    return lax.all_to_all(value, axis, 0, 0, tiled=False)


def per_device(n_row, n_z, n_core, src_feat, tgt_feat):
    width, src_own = src_feat.shape
    tgt_own = tgt_feat.shape[1]
    log_sources = math.log2(src_own * n_row * n_z * n_core)
    log_targets = math.log2(tgt_own * n_z * n_core)
    n_tgt = n_core * tgt_own
    group = n_row * n_core
    x = exchange(call_copies(src_feat, n_z), "z")
    yt = call_prep(lax.all_gather(tgt_feat, "core"))
    e, xa, part = call_first(yt, x, n_z)
    first = exchange(part, "z")
    col_part = call_over_sources(log_targets, e, yt, xa, (group, n_tgt // LANES, LANES), BF16, first)
    col_parts = exchange(col_part, ("row", "core"))
    change = exchange(call_over_targets(log_sources, col_parts, part, e, yt, xa, n_z), "z")
    col_part = call_over_sources(log_targets, e, yt, xa, (group, tgt_own // LANES, LANES), F32, first, change)
    src_pot = call_finish_sources(log_targets, n_tgt, first, change)
    src_pot = lax.all_gather(src_pot, "core", axis=1)
    tgt_pot = call_finish(log_sources, exchange(col_part, ("row", "core")))
    return src_pot.reshape(n_core * n_z * src_own), tgt_pot.reshape(tgt_own)


def solution(mesh):
    n_row, n_col = mesh.shape["row"], mesh.shape["col"]
    n_core = 2
    n_z = n_col // n_core
    fine = Mesh(mesh.devices.reshape(n_row, n_z, n_core), ("row", "z", "core"))
    return jax.shard_map(
        functools.partial(per_device, n_row, n_z, n_core),
        mesh=fine,
        in_specs=(P(None, ("row", "z", "core")), P(None, ("z", "core"))),
        out_specs=(P("row"), P(("z", "core"))),
        check_vma=False,
    )
```

```python
import functools
import math

import jax
import jax.numpy as jnp
from jax import lax
from jax.experimental import pallas as pl
from jax.experimental.pallas import tpu as pltpu
from jax.sharding import Mesh, PartitionSpec as P

INV_EPS = 20.0
EPS = 0.05
LANES = 128
INNER_GAIN = 2.0 * INV_EPS * math.log2(math.e)
SQ_GAIN = -INV_EPS * math.log2(math.e)
FROM_LOG2 = EPS * math.log(2.0)
LOW, HIGH = -91.0, 100.0
F32, BF16 = jnp.float32, jnp.bfloat16
ABOVE, BELOW, SHIFT, SMALL = 14.0, 4.0, -57.0, 2.0**-17


def split3(v):
    hi = v.astype(BF16)
    rest = v - hi.astype(F32)
    mid = rest.astype(BF16)
    return hi, mid, (rest - mid.astype(F32)).astype(BF16)


def bias_rows(v, own, width):
    row = lax.broadcasted_iota(jnp.int32, (width, LANES), 0)
    other = 3 - own
    out = jnp.where((row >= other) & (row < other + 3), 1.0, 0.0)
    for k, term in enumerate(split3(v)):
        out = jnp.where(row == own + k, term.astype(F32), out)
    return out


def prep_targets(y_ref, yt_ref):
    cores, width, own = y_ref.shape
    for c in range(cores):
        for k in range(0, own, LANES):
            y = y_ref[c, :, k : k + LANES].astype(F32)
            sq = jnp.sum(y * y, axis=0, keepdims=True)
            rows = pl.ds(c * own + k, LANES)
            yt_ref[rows, : 2 * width] = jnp.concatenate([y, y], axis=0).T.astype(BF16)
            tail = bias_rows(SQ_GAIN * sq, 0, width)
            yt_ref[rows, 2 * width :] = jnp.concatenate([y, tail], axis=0).T.astype(BF16)


def scores(yt_ref, xa_ref, rows, cols):
    return jnp.dot(yt_ref[rows, :], xa_ref[:, cols], preferred_element_type=F32)


def merge(parts):
    peak = jnp.max(parts, axis=0)
    return peak + jnp.log2(jnp.sum(jnp.exp2(parts - peak[None]), axis=0))


def encode(d):
    size = jnp.abs(d)
    log = jnp.log2(jnp.maximum(size, SMALL))
    t = jnp.exp2(log * jnp.where(log > 0.0, ABOVE, BELOW) + SHIFT)
    t = jnp.where(size < SMALL, 0.0, t)
    return jnp.where(d < 0.0, -t, t).astype(BF16)


def decode(code):
    t = code.astype(F32)
    size = jnp.abs(t)
    log = jnp.log2(jnp.maximum(size, 2.0**-126)) - SHIFT
    d = jnp.exp2(log * jnp.where(log > 0.0, 1.0 / ABOVE, 1.0 / BELOW))
    d = jnp.where(size > 0.0, d, 0.0)
    return jnp.where(t < 0.0, -d, d)


def base_of(d, around):
    a, b, c = (d[..., :1, k : k + 1] + around for k in range(3))
    base = jnp.maximum(jnp.minimum(a, b), jnp.minimum(jnp.maximum(a, b), c))
    at = [lax.broadcasted_iota(jnp.int32, d.shape, d.ndim - k) for k in (2, 1)]
    return base, (at[0] == 0) & (at[1] < 3)


def encode_from_base(value, around):
    head = encode(value - around)
    base, first = base_of(decode(head), around)
    return jnp.where(first, head.astype(F32), encode(value - base).astype(F32)).astype(BF16)


def decode_from_base(code, around):
    d = decode(code)
    base, first = base_of(d, around)
    return jnp.where(first, around, base) + d


def spread_to_rows(v, out_ref):
    for k in range(v.shape[0]):
        out_ref[k * LANES : (k + 1) * LANES, :] = jnp.broadcast_to(v[k : k + 1], (LANES, LANES)).T


def slow_over_targets(yt_ref, xa_ref, pot_ref, out_ref):
    n_tgt = yt_ref.shape[0]
    step = 256

    def one(it, _):
        cols = pl.ds(pl.multiple_of(it * LANES, LANES), LANES)

        def tile(jt):
            rows = pl.ds(pl.multiple_of(jt * step, step), step)
            s = scores(yt_ref, xa_ref, rows, cols)
            return s if pot_ref is None else s + pot_ref[rows, :]

        def peak_step(jt, peak):
            return jnp.maximum(peak, jnp.max(tile(jt), axis=0, keepdims=True))

        peak = lax.fori_loop(0, n_tgt // step, peak_step, jnp.full((1, LANES), -jnp.inf, F32))

        def sum_step(jt, total):
            return total + jnp.sum(jnp.exp2(tile(jt) - peak), axis=0, keepdims=True)

        total = lax.fori_loop(0, n_tgt // step, sum_step, jnp.zeros((1, LANES), F32))
        out_ref[pl.ds(it, 1), :] = peak + jnp.log2(total)
        return 0

    lax.fori_loop(0, out_ref.shape[0], one, 0)


def slow_over_sources(yt_ref, xa_ref, pot_ref, out_ref):
    n_blocks = xa_ref.shape[1] // LANES

    def one(jt, _):
        rows = pl.ds(pl.multiple_of(jt * LANES, LANES), LANES)

        def tile(it):
            cols = pl.ds(pl.multiple_of(it * LANES, LANES), LANES)
            return scores(yt_ref, xa_ref, rows, cols) + pot_ref[pl.ds(it, 1), :]

        def peak_step(it, peak):
            return jnp.maximum(peak, tile(it))

        peak = lax.fori_loop(0, n_blocks, peak_step, jnp.full((LANES, LANES), -jnp.inf, F32))
        peak = jnp.max(peak, axis=1, keepdims=True)

        def sum_step(it, total):
            return total + jnp.exp2(tile(it) - peak)

        total = lax.fori_loop(0, n_blocks, sum_step, jnp.zeros((LANES, LANES), F32))
        value = peak + jnp.log2(jnp.sum(total, axis=1, keepdims=True))
        out_ref[pl.ds(jt, 1), :] = jnp.broadcast_to(value, (LANES, LANES)).T[:1]
        return 0

    lax.fori_loop(0, out_ref.shape[0], one, 0)


def send(value, part_ref):
    copies = part_ref.shape[0]
    part_ref[...] = jnp.broadcast_to(value[None], (copies,) + value.shape)


def first_over_targets(tile, yt_ref, x_ref, e_ref, xa_ref, part_ref, sum_ref):
    n_blocks, width, _ = x_ref.shape
    n_tgt = yt_ref.shape[0]
    n_src = n_blocks * LANES
    for b in range(n_blocks):
        x = x_ref[b].astype(F32)
        sq = jnp.sum(x * x, axis=0, keepdims=True)
        tail = bias_rows(SQ_GAIN * sq, 3, width).astype(BF16)
        xa_ref[:, b * LANES : (b + 1) * LANES] = jnp.concatenate([*split3(INNER_GAIN * x), tail], axis=0)
    acc = jnp.zeros((8, n_src), F32)
    for jt in range(0, n_tgt, tile):
        e = jnp.exp2(scores(yt_ref, xa_ref, pl.ds(jt, tile), slice(None)))
        e_ref[jt : jt + tile, :] = e
        acc = acc + jnp.sum(e.reshape(tile // 8, 8, n_src), axis=0)
    total = jnp.sum(acc, axis=0, keepdims=True)
    for b in range(n_blocks):
        sum_ref[b : b + 1, :] = total[:, b * LANES : (b + 1) * LANES]
    totals = sum_ref[...]
    send(encode_from_base(jnp.log2(totals), math.log2(n_tgt)), part_ref)
    fast = (jnp.min(totals) >= 2.0**LOW) & (jnp.max(totals) <= 2.0**HIGH)

    @pl.when(jnp.logical_not(fast))
    def _():
        slow_over_targets(yt_ref, xa_ref, None, sum_ref)
        send(encode_from_base(sum_ref[...], math.log2(n_tgt)), part_ref)


def checked(totals, pot):
    top = jnp.max(pot)
    floor = jnp.exp2(jnp.minimum(jnp.maximum(top, 0.0), HIGH) + LOW)
    return (top <= HIGH) & (jnp.min(totals) >= floor)


def row_sums(n_tgt, first, *changes):
    return decode_from_base(first, math.log2(n_tgt)) + sum(decode(change) for change in changes)


def over_sources(log_targets, n_parts, *refs):
    parts_refs, refs = refs[:n_parts], refs[n_parts:]
    e_ref, yt_ref, xa_ref, part_ref, sum_ref, pot_ref, yt_buf, xa_buf = refs
    n_tgt, n_src = e_ref.shape
    n_blocks = n_src // LANES
    pot = log_targets - merge(row_sums(n_tgt, *[ref[...] for ref in parts_refs]))
    pot_ref[...] = pot
    u = jnp.exp2(jnp.minimum(pot, HIGH))
    u = [jnp.broadcast_to(u[b : b + 1], (8, LANES)) for b in range(n_blocks)]
    for k in range(n_tgt // LANES):
        block = []
        for r in range(k * LANES, (k + 1) * LANES, 8):
            acc = e_ref[r : r + 8, :LANES] * u[0]
            for b in range(1, n_blocks):
                acc = acc + e_ref[r : r + 8, b * LANES : (b + 1) * LANES] * u[b]
            block.append(acc)
        sum_ref[k : k + 1, :] = jnp.sum(jnp.concatenate(block, axis=0).T, axis=0, keepdims=True)
    totals = sum_ref[...]

    def put(value):
        copies, n, _ = part_ref.shape
        if part_ref.dtype == BF16:
            value = encode(value - math.log2(n_src))
        for k in range(copies):
            at = (k * n) % value.shape[0]
            part_ref[k] = value[at : at + n]

    put(jnp.log2(totals))

    @pl.when(jnp.logical_not(checked(totals, pot)))
    def _():
        pltpu.sync_copy(yt_ref, yt_buf)
        pltpu.sync_copy(xa_ref, xa_buf)
        slow_over_sources(yt_buf, xa_buf, pot_ref, sum_ref)
        put(sum_ref[...])


def over_targets(log_sources, parts_ref, before_ref, e_ref, yt_ref, xa_ref, part_ref, sum_ref, pot_ref, yt_buf, xa_buf):
    n_tgt, n_src = e_ref.shape
    n_blocks = n_src // LANES
    pot = log_sources - merge(math.log2(n_src) + decode(parts_ref[...]))
    u = jnp.exp2(jnp.minimum(pot, HIGH))
    acc = [jnp.zeros((8, LANES), F32)] * n_blocks
    for k in range(n_tgt // LANES):
        v = jnp.broadcast_to(u[k : k + 1], (LANES, LANES)).T
        for r in range(0, LANES, 8):
            at = k * LANES + r
            for b in range(n_blocks):
                acc[b] = acc[b] + e_ref[at : at + 8, b * LANES : (b + 1) * LANES] * v[r : r + 8]
    for b in range(n_blocks):
        sum_ref[b : b + 1, :] = jnp.sum(acc[b], axis=0, keepdims=True)
    totals = sum_ref[...]
    before = row_sums(n_tgt, before_ref[0])
    send(encode(jnp.log2(totals) - before), part_ref)

    @pl.when(jnp.logical_not(checked(totals, pot)))
    def _():
        pltpu.sync_copy(yt_ref, yt_buf)
        pltpu.sync_copy(xa_ref, xa_buf)
        spread_to_rows(pot, pot_ref)
        slow_over_targets(yt_buf, xa_buf, pot_ref, sum_ref)
        send(encode(sum_ref[...] - before), part_ref)


def make_copies(x_ref, out_ref, buf, sems):
    pltpu.sync_copy(x_ref, buf)
    copies = [pltpu.make_async_copy(buf, out_ref.at[k], sems.at[k]) for k in range(out_ref.shape[0])]
    for copy in copies:
        copy.start()
    for copy in copies:
        copy.wait()


def finish_sources(log_targets, n_tgt, first_ref, change_ref, out_ref):
    out_ref[...] = FROM_LOG2 * (log_targets - merge(row_sums(n_tgt, first_ref[...], change_ref[...])))


def finish_targets(log_sources, parts_ref, out_ref):
    out_ref[...] = FROM_LOG2 * (log_sources - merge(parts_ref[...]))


VMEM = pl.BlockSpec(memory_space=pltpu.VMEM)
ANY = pl.BlockSpec(memory_space=pl.ANY)
LIMIT = 20 << 20


def params():
    return pltpu.CompilerParams(vmem_limit_bytes=LIMIT)


def call_prep(y):
    cores, width, own = y.shape
    return pl.pallas_call(
        prep_targets,
        out_shape=jax.ShapeDtypeStruct((cores * own, 4 * width), BF16),
        in_specs=[VMEM],
        out_specs=VMEM,
        compiler_params=params(),
        name="prep_targets",
    )(y)


def call_copies(x, copies):
    return pl.pallas_call(
        make_copies,
        out_shape=pltpu.HBM((copies,) + x.shape, x.dtype),
        in_specs=[ANY],
        out_specs=ANY,
        scratch_shapes=[pltpu.VMEM(x.shape, x.dtype), pltpu.SemaphoreType.DMA((copies,))],
        compiler_params=params(),
        name="make_copies",
    )(pltpu.with_memory_space_constraint(x, pltpu.HBM))


def call_finish_sources(log_targets, n_tgt, first, change):
    return pl.pallas_call(
        functools.partial(finish_sources, log_targets, n_tgt),
        out_shape=jax.ShapeDtypeStruct(first.shape[1:], F32),
        in_specs=[VMEM, VMEM],
        out_specs=VMEM,
        compiler_params=params(),
        name="finish_sources",
    )(first, change)


def call_finish(log_sources, parts):
    return pl.pallas_call(
        functools.partial(finish_targets, log_sources),
        out_shape=jax.ShapeDtypeStruct(parts.shape[1:], F32),
        in_specs=[VMEM],
        out_specs=VMEM,
        compiler_params=params(),
        name="finish_targets",
    )(parts)


def call_first(yt, x, copies, tile=128):
    n_blocks, width, lanes = x.shape
    n_tgt, n_src = yt.shape[0], n_blocks * lanes
    return pl.pallas_call(
        functools.partial(first_over_targets, tile),
        out_shape=(
            pltpu.VMEM((n_tgt, n_src), F32),
            jax.ShapeDtypeStruct((4 * width, n_src), BF16),
            jax.ShapeDtypeStruct((copies, n_blocks, lanes), BF16),
        ),
        in_specs=[VMEM, VMEM],
        out_specs=(VMEM, VMEM, VMEM),
        scratch_shapes=[pltpu.VMEM((n_blocks, lanes), F32)],
        compiler_params=params(),
        name="first_over_targets",
    )(yt, x)


def call_over_sources(log_targets, e, yt, xa, part_shape, part_type, *parts):
    n_tgt, n_src = e.shape
    return pl.pallas_call(
        functools.partial(over_sources, log_targets, len(parts)),
        out_shape=jax.ShapeDtypeStruct(part_shape, part_type),
        in_specs=[VMEM] * len(parts) + [VMEM, ANY, ANY],
        out_specs=VMEM,
        scratch_shapes=[
            pltpu.VMEM((n_tgt // LANES, LANES), F32),
            pltpu.VMEM((n_src // LANES, LANES), F32),
            pltpu.VMEM(yt.shape, BF16),
            pltpu.VMEM(xa.shape, BF16),
        ],
        compiler_params=params(),
        name="over_sources",
    )(*parts, e, yt, xa)


def call_over_targets(log_sources, parts, before, e, yt, xa, copies):
    n_tgt, n_src = e.shape
    return pl.pallas_call(
        functools.partial(over_targets, log_sources),
        out_shape=jax.ShapeDtypeStruct((copies, n_src // LANES, LANES), BF16),
        in_specs=[VMEM, VMEM, VMEM, ANY, ANY],
        out_specs=VMEM,
        scratch_shapes=[
            pltpu.VMEM((n_src // LANES, LANES), F32),
            pltpu.VMEM((n_tgt, LANES), F32),
            pltpu.VMEM(yt.shape, BF16),
            pltpu.VMEM(xa.shape, BF16),
        ],
        compiler_params=params(),
        name="over_targets",
    )(parts, before, e, yt, xa)


def exchange(value, axis):
    return lax.all_to_all(value, axis, 0, 0, tiled=False)


def per_device(n_row, n_z, n_core, src_feat, tgt_feat):
    width, src_own = src_feat.shape
    tgt_own = tgt_feat.shape[1]
    log_sources = math.log2(src_own * n_row * n_z * n_core)
    log_targets = math.log2(tgt_own * n_z * n_core)
    n_tgt = n_core * tgt_own
    group = n_row * n_core
    x = exchange(call_copies(src_feat, n_z), "z")
    yt = call_prep(lax.all_gather(tgt_feat, "core"))
    e, xa, part = call_first(yt, x, n_z)
    first = exchange(part, "z")
    col_part = call_over_sources(log_targets, e, yt, xa, (group, n_tgt // LANES, LANES), BF16, first)
    col_parts = exchange(col_part, ("row", "core"))
    change = exchange(call_over_targets(log_sources, col_parts, part, e, yt, xa, n_z), "z")
    col_part = call_over_sources(log_targets, e, yt, xa, (group, tgt_own // LANES, LANES), F32, first, change)
    src_pot = call_finish_sources(log_targets, n_tgt, first, change)
    src_pot = lax.all_gather(src_pot, "core", axis=1)
    tgt_pot = call_finish(log_sources, exchange(col_part, ("row", "core")))
    return src_pot.reshape(n_core * n_z * src_own), tgt_pot.reshape(tgt_own)


def solution(mesh):
    n_row, n_col = mesh.shape["row"], mesh.shape["col"]
    n_core = 2
    n_z = n_col // n_core
    fine = Mesh(mesh.devices.reshape(n_row, n_z, n_core), ("row", "z", "core"))
    return jax.shard_map(
        functools.partial(per_device, n_row, n_z, n_core),
        mesh=fine,
        in_specs=(P(None, ("row", "z", "core")), P(None, ("z", "core"))),
        out_specs=(P("row"), P(("z", "core"))),
        check_vma=False,
    )
```

```python
import functools
import math

import jax
import jax.numpy as jnp
from jax import lax
from jax.experimental import pallas as pl
from jax.experimental.pallas import tpu as pltpu
from jax.sharding import Mesh, PartitionSpec as P

INV_EPS = 20.0
EPS = 0.05
LANES = 128
INNER_GAIN = 2.0 * INV_EPS * math.log2(math.e)
SQ_GAIN = -INV_EPS * math.log2(math.e)
FROM_LOG2 = EPS * math.log(2.0)
LOW, HIGH = -91.0, 100.0
F32, BF16 = jnp.float32, jnp.bfloat16
LOW_SLOPE, MID_SLOPE, HIGH_SLOPE = 4.0, 18.0, 9.0
KNEE, SHIFT, SMALL = 9.0, -72.0, 2.0**-13
KNEE_HEIGHT = MID_SLOPE * KNEE


def split3(v):
    hi = v.astype(BF16)
    rest = v - hi.astype(F32)
    mid = rest.astype(BF16)
    return hi, mid, (rest - mid.astype(F32)).astype(BF16)


def bias_rows(v, own, width):
    row = lax.broadcasted_iota(jnp.int32, (width, LANES), 0)
    other = 3 - own
    out = jnp.where((row >= other) & (row < other + 3), 1.0, 0.0)
    for k, term in enumerate(split3(v)):
        out = jnp.where(row == own + k, term.astype(F32), out)
    return out


def prep_targets(y_ref, yt_ref):
    cores, width, own = y_ref.shape
    for c in range(cores):
        for k in range(0, own, LANES):
            y = y_ref[c, :, k : k + LANES].astype(F32)
            sq = jnp.sum(y * y, axis=0, keepdims=True)
            rows = pl.ds(c * own + k, LANES)
            yt_ref[rows, : 2 * width] = jnp.concatenate([y, y], axis=0).T.astype(BF16)
            tail = bias_rows(SQ_GAIN * sq, 0, width)
            yt_ref[rows, 2 * width :] = jnp.concatenate([y, tail], axis=0).T.astype(BF16)


def scores(yt_ref, xa_ref, rows, cols):
    return jnp.dot(yt_ref[rows, :], xa_ref[:, cols], preferred_element_type=F32)


def merge(parts):
    peak = jnp.max(parts, axis=0)
    return peak + jnp.log2(jnp.sum(jnp.exp2(parts - peak[None]), axis=0))


def encode(d):
    size = jnp.abs(d)
    log = jnp.log2(jnp.maximum(size, SMALL))
    height = jnp.where(log > KNEE, KNEE_HEIGHT + HIGH_SLOPE * (log - KNEE), jnp.where(log > 0.0, MID_SLOPE, LOW_SLOPE) * log)
    t = jnp.where(size < SMALL, 0.0, jnp.exp2(height + SHIFT))
    return jnp.where(d < 0.0, -t, t).astype(BF16)


def decode(code):
    t = code.astype(F32)
    size = jnp.abs(t)
    height = jnp.log2(jnp.maximum(size, 2.0**-126)) - SHIFT
    low = jnp.where(height > 0.0, 1.0 / MID_SLOPE, 1.0 / LOW_SLOPE) * height
    log = jnp.where(height > KNEE_HEIGHT, KNEE + (height - KNEE_HEIGHT) * (1.0 / HIGH_SLOPE), low)
    d = jnp.where(size > 0.0, jnp.exp2(log), 0.0)
    return jnp.where(t < 0.0, -d, d)


def spread_to_rows(v, out_ref):
    for k in range(v.shape[0]):
        out_ref[k * LANES : (k + 1) * LANES, :] = jnp.broadcast_to(v[k : k + 1], (LANES, LANES)).T


def slow_over_targets(yt_ref, xa_ref, pot_ref, out_ref):
    n_tgt = yt_ref.shape[0]
    step = 256

    def one(it, _):
        cols = pl.ds(pl.multiple_of(it * LANES, LANES), LANES)

        def tile(jt):
            rows = pl.ds(pl.multiple_of(jt * step, step), step)
            s = scores(yt_ref, xa_ref, rows, cols)
            return s if pot_ref is None else s + pot_ref[rows, :]

        def peak_step(jt, peak):
            return jnp.maximum(peak, jnp.max(tile(jt), axis=0, keepdims=True))

        peak = lax.fori_loop(0, n_tgt // step, peak_step, jnp.full((1, LANES), -jnp.inf, F32))

        def sum_step(jt, total):
            return total + jnp.sum(jnp.exp2(tile(jt) - peak), axis=0, keepdims=True)

        total = lax.fori_loop(0, n_tgt // step, sum_step, jnp.zeros((1, LANES), F32))
        out_ref[pl.ds(it, 1), :] = peak + jnp.log2(total)
        return 0

    lax.fori_loop(0, out_ref.shape[0], one, 0)


def slow_over_sources(yt_ref, xa_ref, pot_ref, out_ref):
    n_blocks = xa_ref.shape[1] // LANES

    def one(jt, _):
        rows = pl.ds(pl.multiple_of(jt * LANES, LANES), LANES)

        def tile(it):
            cols = pl.ds(pl.multiple_of(it * LANES, LANES), LANES)
            return scores(yt_ref, xa_ref, rows, cols) + pot_ref[pl.ds(it, 1), :]

        def peak_step(it, peak):
            return jnp.maximum(peak, tile(it))

        peak = lax.fori_loop(0, n_blocks, peak_step, jnp.full((LANES, LANES), -jnp.inf, F32))
        peak = jnp.max(peak, axis=1, keepdims=True)

        def sum_step(it, total):
            return total + jnp.exp2(tile(it) - peak)

        total = lax.fori_loop(0, n_blocks, sum_step, jnp.zeros((LANES, LANES), F32))
        value = peak + jnp.log2(jnp.sum(total, axis=1, keepdims=True))
        out_ref[pl.ds(jt, 1), :] = jnp.broadcast_to(value, (LANES, LANES)).T[:1]
        return 0

    lax.fori_loop(0, out_ref.shape[0], one, 0)


def send(value, part_ref):
    copies = part_ref.shape[0]
    part_ref[...] = jnp.broadcast_to(value[None], (copies,) + value.shape)


def first_over_targets(tile, yt_ref, x_ref, e_ref, xa_ref, part_ref, sum_ref):
    n_blocks, width, _ = x_ref.shape
    n_tgt = yt_ref.shape[0]
    n_src = n_blocks * LANES
    for b in range(n_blocks):
        x = x_ref[b].astype(F32)
        sq = jnp.sum(x * x, axis=0, keepdims=True)
        tail = bias_rows(SQ_GAIN * sq, 3, width).astype(BF16)
        xa_ref[:, b * LANES : (b + 1) * LANES] = jnp.concatenate([*split3(INNER_GAIN * x), tail], axis=0)
    acc = jnp.zeros((8, n_src), F32)
    for jt in range(0, n_tgt, tile):
        e = jnp.exp2(scores(yt_ref, xa_ref, pl.ds(jt, tile), slice(None)))
        e_ref[jt : jt + tile, :] = e
        acc = acc + jnp.sum(e.reshape(tile // 8, 8, n_src), axis=0)
    total = jnp.sum(acc, axis=0, keepdims=True)
    for b in range(n_blocks):
        sum_ref[b : b + 1, :] = total[:, b * LANES : (b + 1) * LANES]
    totals = sum_ref[...]
    send(jnp.log2(totals), part_ref)
    fast = (jnp.min(totals) >= 2.0**LOW) & (jnp.max(totals) <= 2.0**HIGH)

    @pl.when(jnp.logical_not(fast))
    def _():
        slow_over_targets(yt_ref, xa_ref, None, sum_ref)
        send(sum_ref[...], part_ref)


def checked(totals, pot):
    top = jnp.max(pot)
    floor = jnp.exp2(jnp.minimum(jnp.maximum(top, 0.0), HIGH) + LOW)
    return (top <= HIGH) & (jnp.min(totals) >= floor)


def row_sums(first, *changes):
    return first + sum(decode(change) for change in changes)


def over_sources(log_targets, n_parts, *refs):
    parts_refs, refs = refs[:n_parts], refs[n_parts:]
    e_ref, yt_ref, xa_ref, part_ref, sum_ref, pot_ref, yt_buf, xa_buf = refs
    n_tgt, n_src = e_ref.shape
    n_blocks = n_src // LANES
    pot = log_targets - merge(row_sums(*[ref[...] for ref in parts_refs]))
    pot_ref[...] = pot
    u = jnp.exp2(jnp.minimum(pot, HIGH))
    u = [jnp.broadcast_to(u[b : b + 1], (8, LANES)) for b in range(n_blocks)]
    for k in range(n_tgt // LANES):
        block = []
        for r in range(k * LANES, (k + 1) * LANES, 8):
            acc = e_ref[r : r + 8, :LANES] * u[0]
            for b in range(1, n_blocks):
                acc = acc + e_ref[r : r + 8, b * LANES : (b + 1) * LANES] * u[b]
            block.append(acc)
        sum_ref[k : k + 1, :] = jnp.sum(jnp.concatenate(block, axis=0).T, axis=0, keepdims=True)
    totals = sum_ref[...]

    def put(value):
        copies, n, _ = part_ref.shape
        if part_ref.dtype == BF16:
            value = encode(value - math.log2(n_src))
        for k in range(copies):
            at = (k * n) % value.shape[0]
            part_ref[k] = value[at : at + n]

    put(jnp.log2(totals))

    @pl.when(jnp.logical_not(checked(totals, pot)))
    def _():
        pltpu.sync_copy(yt_ref, yt_buf)
        pltpu.sync_copy(xa_ref, xa_buf)
        slow_over_sources(yt_buf, xa_buf, pot_ref, sum_ref)
        put(sum_ref[...])


def over_targets(log_sources, parts_ref, before_ref, e_ref, yt_ref, xa_ref, part_ref, sum_ref, pot_ref, yt_buf, xa_buf):
    n_tgt, n_src = e_ref.shape
    n_blocks = n_src // LANES
    pot = log_sources - merge(math.log2(n_src) + decode(parts_ref[...]))
    u = jnp.exp2(jnp.minimum(pot, HIGH))
    acc = [jnp.zeros((8, LANES), F32)] * n_blocks
    for k in range(n_tgt // LANES):
        v = jnp.broadcast_to(u[k : k + 1], (LANES, LANES)).T
        for r in range(0, LANES, 8):
            at = k * LANES + r
            for b in range(n_blocks):
                acc[b] = acc[b] + e_ref[at : at + 8, b * LANES : (b + 1) * LANES] * v[r : r + 8]
    for b in range(n_blocks):
        sum_ref[b : b + 1, :] = jnp.sum(acc[b], axis=0, keepdims=True)
    totals = sum_ref[...]
    before = before_ref[0]
    send(encode(jnp.log2(totals) - before), part_ref)

    @pl.when(jnp.logical_not(checked(totals, pot)))
    def _():
        pltpu.sync_copy(yt_ref, yt_buf)
        pltpu.sync_copy(xa_ref, xa_buf)
        spread_to_rows(pot, pot_ref)
        slow_over_targets(yt_buf, xa_buf, pot_ref, sum_ref)
        send(encode(sum_ref[...] - before), part_ref)


def make_copies(x_ref, out_ref, buf, sems):
    pltpu.sync_copy(x_ref, buf)
    copies = [pltpu.make_async_copy(buf, out_ref.at[k], sems.at[k]) for k in range(out_ref.shape[0])]
    for copy in copies:
        copy.start()
    for copy in copies:
        copy.wait()


def finish_sources(log_targets, first_ref, change_ref, out_ref):
    out_ref[...] = FROM_LOG2 * (log_targets - merge(row_sums(first_ref[...], change_ref[...])))


def finish_targets(log_sources, parts_ref, out_ref):
    out_ref[...] = FROM_LOG2 * (log_sources - merge(parts_ref[...]))


VMEM = pl.BlockSpec(memory_space=pltpu.VMEM)
ANY = pl.BlockSpec(memory_space=pl.ANY)
LIMIT = 20 << 20


def params():
    return pltpu.CompilerParams(vmem_limit_bytes=LIMIT)


def call_prep(y):
    cores, width, own = y.shape
    return pl.pallas_call(
        prep_targets,
        out_shape=jax.ShapeDtypeStruct((cores * own, 4 * width), BF16),
        in_specs=[VMEM],
        out_specs=VMEM,
        compiler_params=params(),
        name="prep_targets",
    )(y)


def call_copies(x, copies):
    return pl.pallas_call(
        make_copies,
        out_shape=pltpu.HBM((copies,) + x.shape, x.dtype),
        in_specs=[ANY],
        out_specs=ANY,
        scratch_shapes=[pltpu.VMEM(x.shape, x.dtype), pltpu.SemaphoreType.DMA((copies,))],
        compiler_params=params(),
        name="make_copies",
    )(pltpu.with_memory_space_constraint(x, pltpu.HBM))


def call_finish_sources(log_targets, first, change):
    return pl.pallas_call(
        functools.partial(finish_sources, log_targets),
        out_shape=jax.ShapeDtypeStruct(first.shape[1:], F32),
        in_specs=[VMEM, VMEM],
        out_specs=VMEM,
        compiler_params=params(),
        name="finish_sources",
    )(first, change)


def call_finish(log_sources, parts):
    return pl.pallas_call(
        functools.partial(finish_targets, log_sources),
        out_shape=jax.ShapeDtypeStruct(parts.shape[1:], F32),
        in_specs=[VMEM],
        out_specs=VMEM,
        compiler_params=params(),
        name="finish_targets",
    )(parts)


def call_first(yt, x, copies, tile=128):
    n_blocks, width, lanes = x.shape
    n_tgt, n_src = yt.shape[0], n_blocks * lanes
    return pl.pallas_call(
        functools.partial(first_over_targets, tile),
        out_shape=(
            pltpu.VMEM((n_tgt, n_src), F32),
            jax.ShapeDtypeStruct((4 * width, n_src), BF16),
            jax.ShapeDtypeStruct((copies, n_blocks, lanes), F32),
        ),
        in_specs=[VMEM, VMEM],
        out_specs=(VMEM, VMEM, VMEM),
        scratch_shapes=[pltpu.VMEM((n_blocks, lanes), F32)],
        compiler_params=params(),
        name="first_over_targets",
    )(yt, x)


def call_over_sources(log_targets, e, yt, xa, part_shape, part_type, *parts):
    n_tgt, n_src = e.shape
    return pl.pallas_call(
        functools.partial(over_sources, log_targets, len(parts)),
        out_shape=jax.ShapeDtypeStruct(part_shape, part_type),
        in_specs=[VMEM] * len(parts) + [VMEM, ANY, ANY],
        out_specs=VMEM,
        scratch_shapes=[
            pltpu.VMEM((n_tgt // LANES, LANES), F32),
            pltpu.VMEM((n_src // LANES, LANES), F32),
            pltpu.VMEM(yt.shape, BF16),
            pltpu.VMEM(xa.shape, BF16),
        ],
        compiler_params=params(),
        name="over_sources",
    )(*parts, e, yt, xa)


def call_over_targets(log_sources, parts, before, e, yt, xa, copies):
    n_tgt, n_src = e.shape
    return pl.pallas_call(
        functools.partial(over_targets, log_sources),
        out_shape=jax.ShapeDtypeStruct((copies, n_src // LANES, LANES), BF16),
        in_specs=[VMEM, VMEM, VMEM, ANY, ANY],
        out_specs=VMEM,
        scratch_shapes=[
            pltpu.VMEM((n_src // LANES, LANES), F32),
            pltpu.VMEM((n_tgt, LANES), F32),
            pltpu.VMEM(yt.shape, BF16),
            pltpu.VMEM(xa.shape, BF16),
        ],
        compiler_params=params(),
        name="over_targets",
    )(parts, before, e, yt, xa)


def exchange(value, axis):
    return lax.all_to_all(value, axis, 0, 0, tiled=False)


def per_device(n_row, n_z, n_core, src_feat, tgt_feat):
    width, src_own = src_feat.shape
    tgt_own = tgt_feat.shape[1]
    log_sources = math.log2(src_own * n_row * n_z * n_core)
    log_targets = math.log2(tgt_own * n_z * n_core)
    n_tgt = n_core * tgt_own
    group = n_row * n_core
    x = exchange(call_copies(src_feat, n_z), "z")
    yt = call_prep(lax.all_gather(tgt_feat, "core"))
    e, xa, part = call_first(yt, x, n_z)
    first = exchange(part, "z")
    col_part = call_over_sources(log_targets, e, yt, xa, (group, n_tgt // LANES, LANES), BF16, first)
    col_parts = exchange(col_part, ("row", "core"))
    change = exchange(call_over_targets(log_sources, col_parts, part, e, yt, xa, n_z), "z")
    col_part = call_over_sources(log_targets, e, yt, xa, (group, tgt_own // LANES, LANES), F32, first, change)
    src_pot = call_finish_sources(log_targets, first, change)
    src_pot = lax.all_gather(src_pot, "core", axis=1)
    tgt_pot = call_finish(log_sources, exchange(col_part, ("row", "core")))
    return src_pot.reshape(n_core * n_z * src_own), tgt_pot.reshape(tgt_own)


def solution(mesh):
    n_row, n_col = mesh.shape["row"], mesh.shape["col"]
    n_core = 2
    n_z = n_col // n_core
    fine = Mesh(mesh.devices.reshape(n_row, n_z, n_core), ("row", "z", "core"))
    return jax.shard_map(
        functools.partial(per_device, n_row, n_z, n_core),
        mesh=fine,
        in_specs=(P(None, ("row", "z", "core")), P(None, ("z", "core"))),
        out_specs=(P("row"), P(("z", "core"))),
        check_vma=False,
    )
```

```python
import functools
import math

import jax
import jax.numpy as jnp
from jax import lax
from jax.experimental import pallas as pl
from jax.experimental.pallas import tpu as pltpu
from jax.sharding import Mesh, PartitionSpec as P

INV_EPS = 20.0
EPS = 0.05
LANES = 128
INNER_GAIN = 2.0 * INV_EPS * math.log2(math.e)
SQ_GAIN = -INV_EPS * math.log2(math.e)
FROM_LOG2 = EPS * math.log(2.0)
LOW, HIGH = -91.0, 100.0
F32, BF16 = jnp.float32, jnp.bfloat16
LOW_SLOPE, MID_SLOPE, HIGH_SLOPE = 4.0, 18.0, 9.0
KNEE, SHIFT, SMALL = 9.0, -72.0, 2.0**-13
KNEE_HEIGHT = MID_SLOPE * KNEE


def split3(v):
    hi = v.astype(BF16)
    rest = v - hi.astype(F32)
    mid = rest.astype(BF16)
    return hi, mid, (rest - mid.astype(F32)).astype(BF16)


def bias_rows(v, own, width):
    row = lax.broadcasted_iota(jnp.int32, (width, LANES), 0)
    other = 3 - own
    out = jnp.where((row >= other) & (row < other + 3), 1.0, 0.0)
    for k, term in enumerate(split3(v)):
        out = jnp.where(row == own + k, term.astype(F32), out)
    return out


def prep_targets(y_ref, yt_ref):
    cores, width, own = y_ref.shape
    for c in range(cores):
        for k in range(0, own, LANES):
            y = y_ref[c, :, k : k + LANES].astype(F32)
            sq = jnp.sum(y * y, axis=0, keepdims=True)
            rows = pl.ds(c * own + k, LANES)
            yt_ref[rows, : 2 * width] = jnp.concatenate([y, y], axis=0).T.astype(BF16)
            tail = bias_rows(SQ_GAIN * sq, 0, width)
            yt_ref[rows, 2 * width :] = jnp.concatenate([y, tail], axis=0).T.astype(BF16)


def scores(yt_ref, xa_ref, rows, cols):
    return jnp.dot(yt_ref[rows, :], xa_ref[:, cols], preferred_element_type=F32)


def merge(parts):
    peak = jnp.max(parts, axis=0)
    return peak + jnp.log2(jnp.sum(jnp.exp2(parts - peak[None]), axis=0))


def encode(d):
    size = jnp.abs(d)
    log = jnp.log2(jnp.maximum(size, SMALL))
    height = jnp.where(log > KNEE, KNEE_HEIGHT + HIGH_SLOPE * (log - KNEE), jnp.where(log > 0.0, MID_SLOPE, LOW_SLOPE) * log)
    t = jnp.where(size < SMALL, 0.0, jnp.exp2(height + SHIFT))
    return jnp.where(d < 0.0, -t, t).astype(BF16)


def decode(code):
    t = code.astype(F32)
    size = jnp.abs(t)
    height = jnp.log2(jnp.maximum(size, 2.0**-126)) - SHIFT
    low = jnp.where(height > 0.0, 1.0 / MID_SLOPE, 1.0 / LOW_SLOPE) * height
    log = jnp.where(height > KNEE_HEIGHT, KNEE + (height - KNEE_HEIGHT) * (1.0 / HIGH_SLOPE), low)
    d = jnp.where(size > 0.0, jnp.exp2(log), 0.0)
    return jnp.where(t < 0.0, -d, d)


def finest(d):
    size = jnp.abs(d)
    slope = jnp.where(size < 1.02, 1.0 / LOW_SLOPE, jnp.where(size > 0.98 * 2.0**KNEE, 1.0 / HIGH_SLOPE, 1.0 / MID_SLOPE))
    return jnp.maximum(size * slope * (1.1 * 2.0**-8), 1.05 * SMALL)


def pack(d):
    n = d.shape[0]
    code = encode(d)
    near = decode(code)
    lost = jnp.clip((d - near) / finest(near), -1.0, 1.0)
    level = jnp.floor((lost + 1.0) * 63.5 + 0.5)
    pair = jnp.exp2(level[: n // 2] - 64.0) * (1.0 + level[n // 2 :] * (1.0 / 128.0))
    return jnp.concatenate([code.astype(F32), pair], axis=0).astype(BF16)


def unpack(packed):
    values = packed.astype(F32)
    n = values.shape[-2] * 2 // 3
    near, pair = decode(values[..., :n, :]), values[..., n:, :]
    exponent = jnp.floor(jnp.log2(pair * (1.0 + 2.0**-9)))
    level = jnp.concatenate([exponent + 64.0, (pair * jnp.exp2(-exponent) - 1.0) * 128.0], axis=-2)
    return near + (level * (1.0 / 63.5) - 1.0) * finest(near)


def spread_to_rows(v, out_ref):
    for k in range(v.shape[0]):
        out_ref[k * LANES : (k + 1) * LANES, :] = jnp.broadcast_to(v[k : k + 1], (LANES, LANES)).T


def slow_over_targets(yt_ref, xa_ref, pot_ref, out_ref):
    n_tgt = yt_ref.shape[0]
    step = 256

    def one(it, _):
        cols = pl.ds(pl.multiple_of(it * LANES, LANES), LANES)

        def tile(jt):
            rows = pl.ds(pl.multiple_of(jt * step, step), step)
            s = scores(yt_ref, xa_ref, rows, cols)
            return s if pot_ref is None else s + pot_ref[rows, :]

        def peak_step(jt, peak):
            return jnp.maximum(peak, jnp.max(tile(jt), axis=0, keepdims=True))

        peak = lax.fori_loop(0, n_tgt // step, peak_step, jnp.full((1, LANES), -jnp.inf, F32))

        def sum_step(jt, total):
            return total + jnp.sum(jnp.exp2(tile(jt) - peak), axis=0, keepdims=True)

        total = lax.fori_loop(0, n_tgt // step, sum_step, jnp.zeros((1, LANES), F32))
        out_ref[pl.ds(it, 1), :] = peak + jnp.log2(total)
        return 0

    lax.fori_loop(0, out_ref.shape[0], one, 0)


def slow_over_sources(yt_ref, xa_ref, pot_ref, out_ref):
    n_blocks = xa_ref.shape[1] // LANES

    def one(jt, _):
        rows = pl.ds(pl.multiple_of(jt * LANES, LANES), LANES)

        def tile(it):
            cols = pl.ds(pl.multiple_of(it * LANES, LANES), LANES)
            return scores(yt_ref, xa_ref, rows, cols) + pot_ref[pl.ds(it, 1), :]

        def peak_step(it, peak):
            return jnp.maximum(peak, tile(it))

        peak = lax.fori_loop(0, n_blocks, peak_step, jnp.full((LANES, LANES), -jnp.inf, F32))
        peak = jnp.max(peak, axis=1, keepdims=True)

        def sum_step(it, total):
            return total + jnp.exp2(tile(it) - peak)

        total = lax.fori_loop(0, n_blocks, sum_step, jnp.zeros((LANES, LANES), F32))
        value = peak + jnp.log2(jnp.sum(total, axis=1, keepdims=True))
        out_ref[pl.ds(jt, 1), :] = jnp.broadcast_to(value, (LANES, LANES)).T[:1]
        return 0

    lax.fori_loop(0, out_ref.shape[0], one, 0)


def send(value, part_ref):
    copies = part_ref.shape[0]
    part_ref[...] = jnp.broadcast_to(value[None], (copies,) + value.shape)


def first_over_targets(tile, yt_ref, x_ref, e_ref, xa_ref, part_ref, sum_ref):
    n_blocks, width, _ = x_ref.shape
    n_tgt = yt_ref.shape[0]
    n_src = n_blocks * LANES
    for b in range(n_blocks):
        x = x_ref[b].astype(F32)
        sq = jnp.sum(x * x, axis=0, keepdims=True)
        tail = bias_rows(SQ_GAIN * sq, 3, width).astype(BF16)
        xa_ref[:, b * LANES : (b + 1) * LANES] = jnp.concatenate([*split3(INNER_GAIN * x), tail], axis=0)
    acc = jnp.zeros((8, n_src), F32)
    for jt in range(0, n_tgt, tile):
        e = jnp.exp2(scores(yt_ref, xa_ref, pl.ds(jt, tile), slice(None)))
        e_ref[jt : jt + tile, :] = e
        acc = acc + jnp.sum(e.reshape(tile // 8, 8, n_src), axis=0)
    total = jnp.sum(acc, axis=0, keepdims=True)
    for b in range(n_blocks):
        sum_ref[b : b + 1, :] = total[:, b * LANES : (b + 1) * LANES]
    totals = sum_ref[...]
    send(pack(jnp.log2(totals) - math.log2(n_tgt)), part_ref)
    fast = (jnp.min(totals) >= 2.0**LOW) & (jnp.max(totals) <= 2.0**HIGH)

    @pl.when(jnp.logical_not(fast))
    def _():
        slow_over_targets(yt_ref, xa_ref, None, sum_ref)
        send(pack(sum_ref[...] - math.log2(n_tgt)), part_ref)


def checked(totals, pot):
    top = jnp.max(pot)
    floor = jnp.exp2(jnp.minimum(jnp.maximum(top, 0.0), HIGH) + LOW)
    return (top <= HIGH) & (jnp.min(totals) >= floor)


def row_sums(n_tgt, first, *changes):
    return math.log2(n_tgt) + unpack(first) + sum(decode(change) for change in changes)


def over_sources(log_targets, n_parts, *refs):
    parts_refs, refs = refs[:n_parts], refs[n_parts:]
    e_ref, yt_ref, xa_ref, part_ref, sum_ref, pot_ref, yt_buf, xa_buf = refs
    n_tgt, n_src = e_ref.shape
    n_blocks = n_src // LANES
    pot = log_targets - merge(row_sums(n_tgt, *[ref[...] for ref in parts_refs]))
    pot_ref[...] = pot
    u = jnp.exp2(jnp.minimum(pot, HIGH))
    u = [jnp.broadcast_to(u[b : b + 1], (8, LANES)) for b in range(n_blocks)]
    for k in range(n_tgt // LANES):
        block = []
        for r in range(k * LANES, (k + 1) * LANES, 8):
            acc = e_ref[r : r + 8, :LANES] * u[0]
            for b in range(1, n_blocks):
                acc = acc + e_ref[r : r + 8, b * LANES : (b + 1) * LANES] * u[b]
            block.append(acc)
        sum_ref[k : k + 1, :] = jnp.sum(jnp.concatenate(block, axis=0).T, axis=0, keepdims=True)
    totals = sum_ref[...]

    def put(value):
        copies, n, _ = part_ref.shape
        if part_ref.dtype == BF16:
            value = encode(value - math.log2(n_src))
        for k in range(copies):
            at = (k * n) % value.shape[0]
            part_ref[k] = value[at : at + n]

    put(jnp.log2(totals))

    @pl.when(jnp.logical_not(checked(totals, pot)))
    def _():
        pltpu.sync_copy(yt_ref, yt_buf)
        pltpu.sync_copy(xa_ref, xa_buf)
        slow_over_sources(yt_buf, xa_buf, pot_ref, sum_ref)
        put(sum_ref[...])


def over_targets(log_sources, parts_ref, before_ref, e_ref, yt_ref, xa_ref, part_ref, sum_ref, pot_ref, yt_buf, xa_buf):
    n_tgt, n_src = e_ref.shape
    n_blocks = n_src // LANES
    pot = log_sources - merge(math.log2(n_src) + decode(parts_ref[...]))
    u = jnp.exp2(jnp.minimum(pot, HIGH))
    acc = [jnp.zeros((8, LANES), F32)] * n_blocks
    for k in range(n_tgt // LANES):
        v = jnp.broadcast_to(u[k : k + 1], (LANES, LANES)).T
        for r in range(0, LANES, 8):
            at = k * LANES + r
            for b in range(n_blocks):
                acc[b] = acc[b] + e_ref[at : at + 8, b * LANES : (b + 1) * LANES] * v[r : r + 8]
    for b in range(n_blocks):
        sum_ref[b : b + 1, :] = jnp.sum(acc[b], axis=0, keepdims=True)
    totals = sum_ref[...]
    before = row_sums(n_tgt, before_ref[0])
    send(encode(jnp.log2(totals) - before), part_ref)

    @pl.when(jnp.logical_not(checked(totals, pot)))
    def _():
        pltpu.sync_copy(yt_ref, yt_buf)
        pltpu.sync_copy(xa_ref, xa_buf)
        spread_to_rows(pot, pot_ref)
        slow_over_targets(yt_buf, xa_buf, pot_ref, sum_ref)
        send(encode(sum_ref[...] - before), part_ref)


def make_copies(x_ref, out_ref, buf, sems):
    pltpu.sync_copy(x_ref, buf)
    copies = [pltpu.make_async_copy(buf, out_ref.at[k], sems.at[k]) for k in range(out_ref.shape[0])]
    for copy in copies:
        copy.start()
    for copy in copies:
        copy.wait()


def finish_sources(log_targets, n_tgt, first_ref, change_ref, out_ref):
    out_ref[...] = FROM_LOG2 * (log_targets - merge(row_sums(n_tgt, first_ref[...], change_ref[...])))


def finish_targets(log_sources, parts_ref, out_ref):
    out_ref[...] = FROM_LOG2 * (log_sources - merge(parts_ref[...]))


VMEM = pl.BlockSpec(memory_space=pltpu.VMEM)
ANY = pl.BlockSpec(memory_space=pl.ANY)
LIMIT = 20 << 20


def params():
    return pltpu.CompilerParams(vmem_limit_bytes=LIMIT)


def call_prep(y):
    cores, width, own = y.shape
    return pl.pallas_call(
        prep_targets,
        out_shape=jax.ShapeDtypeStruct((cores * own, 4 * width), BF16),
        in_specs=[VMEM],
        out_specs=VMEM,
        compiler_params=params(),
        name="prep_targets",
    )(y)


def call_copies(x, copies):
    return pl.pallas_call(
        make_copies,
        out_shape=pltpu.HBM((copies,) + x.shape, x.dtype),
        in_specs=[ANY],
        out_specs=ANY,
        scratch_shapes=[pltpu.VMEM(x.shape, x.dtype), pltpu.SemaphoreType.DMA((copies,))],
        compiler_params=params(),
        name="make_copies",
    )(pltpu.with_memory_space_constraint(x, pltpu.HBM))


def call_finish_sources(log_targets, n_tgt, first, change):
    return pl.pallas_call(
        functools.partial(finish_sources, log_targets, n_tgt),
        out_shape=jax.ShapeDtypeStruct(change.shape[1:], F32),
        in_specs=[VMEM, VMEM],
        out_specs=VMEM,
        compiler_params=params(),
        name="finish_sources",
    )(first, change)


def call_finish(log_sources, parts):
    return pl.pallas_call(
        functools.partial(finish_targets, log_sources),
        out_shape=jax.ShapeDtypeStruct(parts.shape[1:], F32),
        in_specs=[VMEM],
        out_specs=VMEM,
        compiler_params=params(),
        name="finish_targets",
    )(parts)


def call_first(yt, x, copies, tile=128):
    n_blocks, width, lanes = x.shape
    n_tgt, n_src = yt.shape[0], n_blocks * lanes
    return pl.pallas_call(
        functools.partial(first_over_targets, tile),
        out_shape=(
            pltpu.VMEM((n_tgt, n_src), F32),
            jax.ShapeDtypeStruct((4 * width, n_src), BF16),
            jax.ShapeDtypeStruct((copies, n_blocks + n_blocks // 2, lanes), BF16),
        ),
        in_specs=[VMEM, VMEM],
        out_specs=(VMEM, VMEM, VMEM),
        scratch_shapes=[pltpu.VMEM((n_blocks, lanes), F32)],
        compiler_params=params(),
        name="first_over_targets",
    )(yt, x)


def call_over_sources(log_targets, e, yt, xa, part_shape, part_type, *parts):
    n_tgt, n_src = e.shape
    return pl.pallas_call(
        functools.partial(over_sources, log_targets, len(parts)),
        out_shape=jax.ShapeDtypeStruct(part_shape, part_type),
        in_specs=[VMEM] * len(parts) + [VMEM, ANY, ANY],
        out_specs=VMEM,
        scratch_shapes=[
            pltpu.VMEM((n_tgt // LANES, LANES), F32),
            pltpu.VMEM((n_src // LANES, LANES), F32),
            pltpu.VMEM(yt.shape, BF16),
            pltpu.VMEM(xa.shape, BF16),
        ],
        compiler_params=params(),
        name="over_sources",
    )(*parts, e, yt, xa)


def call_over_targets(log_sources, parts, before, e, yt, xa, copies):
    n_tgt, n_src = e.shape
    return pl.pallas_call(
        functools.partial(over_targets, log_sources),
        out_shape=jax.ShapeDtypeStruct((copies, n_src // LANES, LANES), BF16),
        in_specs=[VMEM, VMEM, VMEM, ANY, ANY],
        out_specs=VMEM,
        scratch_shapes=[
            pltpu.VMEM((n_src // LANES, LANES), F32),
            pltpu.VMEM((n_tgt, LANES), F32),
            pltpu.VMEM(yt.shape, BF16),
            pltpu.VMEM(xa.shape, BF16),
        ],
        compiler_params=params(),
        name="over_targets",
    )(parts, before, e, yt, xa)


def exchange(value, axis):
    return lax.all_to_all(value, axis, 0, 0, tiled=False)


def per_device(n_row, n_z, n_core, src_feat, tgt_feat):
    width, src_own = src_feat.shape
    tgt_own = tgt_feat.shape[1]
    log_sources = math.log2(src_own * n_row * n_z * n_core)
    log_targets = math.log2(tgt_own * n_z * n_core)
    n_tgt = n_core * tgt_own
    group = n_row * n_core
    x = exchange(call_copies(src_feat, n_z), "z")
    yt = call_prep(lax.all_gather(tgt_feat, "core"))
    e, xa, part = call_first(yt, x, n_z)
    first = exchange(part, "z")
    col_part = call_over_sources(log_targets, e, yt, xa, (group, n_tgt // LANES, LANES), BF16, first)
    col_parts = exchange(col_part, ("row", "core"))
    change = exchange(call_over_targets(log_sources, col_parts, part, e, yt, xa, n_z), "z")
    col_part = call_over_sources(log_targets, e, yt, xa, (group, tgt_own // LANES, LANES), F32, first, change)
    src_pot = call_finish_sources(log_targets, n_tgt, first, change)
    src_pot = lax.all_gather(src_pot, "core", axis=1)
    tgt_pot = call_finish(log_sources, exchange(col_part, ("row", "core")))
    return src_pot.reshape(n_core * n_z * src_own), tgt_pot.reshape(tgt_own)


def solution(mesh):
    n_row, n_col = mesh.shape["row"], mesh.shape["col"]
    n_core = 2
    n_z = n_col // n_core
    fine = Mesh(mesh.devices.reshape(n_row, n_z, n_core), ("row", "z", "core"))
    return jax.shard_map(
        functools.partial(per_device, n_row, n_z, n_core),
        mesh=fine,
        in_specs=(P(None, ("row", "z", "core")), P(None, ("z", "core"))),
        out_specs=(P("row"), P(("z", "core"))),
        check_vma=False,
    )
```

```python
import functools
import math

import jax
import jax.numpy as jnp
from jax import lax
from jax.experimental import pallas as pl
from jax.experimental.pallas import tpu as pltpu
from jax.sharding import Mesh, PartitionSpec as P

INV_EPS = 20.0
EPS = 0.05
LANES = 128
INNER_GAIN = 2.0 * INV_EPS * math.log2(math.e)
SQ_GAIN = -INV_EPS * math.log2(math.e)
FROM_LOG2 = EPS * math.log(2.0)
LOW, HIGH = -91.0, 100.0
F32, BF16 = jnp.float32, jnp.bfloat16
LOW_SLOPE, MID_SLOPE, HIGH_SLOPE = 4.0, 18.0, 9.0
KNEE, SHIFT, SMALL = 9.0, -72.0, 2.0**-13
KNEE_HEIGHT = MID_SLOPE * KNEE


def split3(v):
    hi = v.astype(BF16)
    rest = v - hi.astype(F32)
    mid = rest.astype(BF16)
    return hi, mid, (rest - mid.astype(F32)).astype(BF16)


def bias_rows(v, own, width):
    row = lax.broadcasted_iota(jnp.int32, (width, LANES), 0)
    other = 3 - own
    out = jnp.where((row >= other) & (row < other + 3), 1.0, 0.0)
    for k, term in enumerate(split3(v)):
        out = jnp.where(row == own + k, term.astype(F32), out)
    return out


def prep_targets(y_ref, yt_ref):
    cores, width, own = y_ref.shape
    for c in range(cores):
        for k in range(0, own, LANES):
            y = y_ref[c, :, k : k + LANES].astype(F32)
            sq = jnp.sum(y * y, axis=0, keepdims=True)
            rows = pl.ds(c * own + k, LANES)
            yt_ref[rows, : 2 * width] = jnp.concatenate([y, y], axis=0).T.astype(BF16)
            tail = bias_rows(SQ_GAIN * sq, 0, width)
            yt_ref[rows, 2 * width :] = jnp.concatenate([y, tail], axis=0).T.astype(BF16)


def scores(yt_ref, xa_ref, rows, cols):
    return jnp.dot(yt_ref[rows, :], xa_ref[:, cols], preferred_element_type=F32)


def merge(parts):
    peak = jnp.max(parts, axis=0)
    return peak + jnp.log2(jnp.sum(jnp.exp2(parts - peak[None]), axis=0))


def encode(d):
    size = jnp.abs(d)
    log = jnp.log2(jnp.maximum(size, SMALL))
    height = jnp.where(log > KNEE, KNEE_HEIGHT + HIGH_SLOPE * (log - KNEE), jnp.where(log > 0.0, MID_SLOPE, LOW_SLOPE) * log)
    t = jnp.where(size < SMALL, 0.0, jnp.exp2(height + SHIFT))
    return jnp.where(d < 0.0, -t, t).astype(BF16)


def decode(code):
    t = code.astype(F32)
    size = jnp.abs(t)
    height = jnp.log2(jnp.maximum(size, 2.0**-126)) - SHIFT
    low = jnp.where(height > 0.0, 1.0 / MID_SLOPE, 1.0 / LOW_SLOPE) * height
    log = jnp.where(height > KNEE_HEIGHT, KNEE + (height - KNEE_HEIGHT) * (1.0 / HIGH_SLOPE), low)
    d = jnp.where(size > 0.0, jnp.exp2(log), 0.0)
    return jnp.where(t < 0.0, -d, d)


def finest(d):
    size = jnp.abs(d)
    slope = jnp.where(size < 1.02, 1.0 / LOW_SLOPE, jnp.where(size > 0.98 * 2.0**KNEE, 1.0 / HIGH_SLOPE, 1.0 / MID_SLOPE))
    return jnp.maximum(size * slope * (1.1 * 2.0**-8), 1.05 * SMALL)


def pack(d):
    n = d.shape[0]
    code = encode(d)
    near = decode(code)
    lost = jnp.clip((d - near) / finest(near), -1.0, 1.0)
    level = jnp.floor((lost + 1.0) * 63.5 + 0.5)
    pair = jnp.exp2(level[: n // 2] - 64.0) * (1.0 + level[n // 2 :] * (1.0 / 128.0))
    return jnp.concatenate([code.astype(F32), pair], axis=0).astype(BF16)


def unpack(packed):
    values = packed.astype(F32)
    n = values.shape[-2] * 2 // 3
    near, pair = decode(values[..., :n, :]), values[..., n:, :]
    exponent = jnp.floor(jnp.log2(pair * (1.0 + 2.0**-9)))
    level = jnp.concatenate([exponent + 64.0, (pair * jnp.exp2(-exponent) - 1.0) * 128.0], axis=-2)
    return near + (level * (1.0 / 63.5) - 1.0) * finest(near)


def spread_to_rows(v, out_ref):
    for k in range(v.shape[0]):
        out_ref[k * LANES : (k + 1) * LANES, :] = jnp.broadcast_to(v[k : k + 1], (LANES, LANES)).T


def slow_over_targets(yt_ref, xa_ref, pot_ref, out_ref):
    n_tgt = yt_ref.shape[0]
    step = 256

    def one(it, _):
        cols = pl.ds(pl.multiple_of(it * LANES, LANES), LANES)

        def tile(jt):
            rows = pl.ds(pl.multiple_of(jt * step, step), step)
            s = scores(yt_ref, xa_ref, rows, cols)
            return s if pot_ref is None else s + pot_ref[rows, :]

        def peak_step(jt, peak):
            return jnp.maximum(peak, jnp.max(tile(jt), axis=0, keepdims=True))

        peak = lax.fori_loop(0, n_tgt // step, peak_step, jnp.full((1, LANES), -jnp.inf, F32))

        def sum_step(jt, total):
            return total + jnp.sum(jnp.exp2(tile(jt) - peak), axis=0, keepdims=True)

        total = lax.fori_loop(0, n_tgt // step, sum_step, jnp.zeros((1, LANES), F32))
        out_ref[pl.ds(it, 1), :] = peak + jnp.log2(total)
        return 0

    lax.fori_loop(0, out_ref.shape[0], one, 0)


def slow_over_sources(yt_ref, xa_ref, pot_ref, out_ref):
    n_blocks = xa_ref.shape[1] // LANES

    def one(jt, _):
        rows = pl.ds(pl.multiple_of(jt * LANES, LANES), LANES)

        def tile(it):
            cols = pl.ds(pl.multiple_of(it * LANES, LANES), LANES)
            return scores(yt_ref, xa_ref, rows, cols) + pot_ref[pl.ds(it, 1), :]

        def peak_step(it, peak):
            return jnp.maximum(peak, tile(it))

        peak = lax.fori_loop(0, n_blocks, peak_step, jnp.full((LANES, LANES), -jnp.inf, F32))
        peak = jnp.max(peak, axis=1, keepdims=True)

        def sum_step(it, total):
            return total + jnp.exp2(tile(it) - peak)

        total = lax.fori_loop(0, n_blocks, sum_step, jnp.zeros((LANES, LANES), F32))
        value = peak + jnp.log2(jnp.sum(total, axis=1, keepdims=True))
        out_ref[pl.ds(jt, 1), :] = jnp.broadcast_to(value, (LANES, LANES)).T[:1]
        return 0

    lax.fori_loop(0, out_ref.shape[0], one, 0)


def send(value, part_ref):
    copies = part_ref.shape[0]
    part_ref[...] = jnp.broadcast_to(value[None], (copies,) + value.shape)


def first_over_targets(tile, yt_ref, x_ref, e_ref, xa_ref, part_ref, sum_ref):
    n_blocks, width, _ = x_ref.shape
    n_tgt = yt_ref.shape[0]
    n_src = n_blocks * LANES
    for b in range(n_blocks):
        x = x_ref[b].astype(F32)
        sq = jnp.sum(x * x, axis=0, keepdims=True)
        tail = bias_rows(SQ_GAIN * sq, 3, width).astype(BF16)
        xa_ref[:, b * LANES : (b + 1) * LANES] = jnp.concatenate([*split3(INNER_GAIN * x), tail], axis=0)
    acc = jnp.zeros((8, n_src), F32)
    for jt in range(0, n_tgt, tile):
        e = jnp.exp2(scores(yt_ref, xa_ref, pl.ds(jt, tile), slice(None)))
        e_ref[jt : jt + tile, :] = e
        acc = acc + jnp.sum(e.reshape(tile // 8, 8, n_src), axis=0)
    total = jnp.sum(acc, axis=0, keepdims=True)
    for b in range(n_blocks):
        sum_ref[b : b + 1, :] = total[:, b * LANES : (b + 1) * LANES]
    totals = sum_ref[...]
    send(pack(jnp.log2(totals) - math.log2(n_tgt)), part_ref)
    fast = (jnp.min(totals) >= 2.0**LOW) & (jnp.max(totals) <= 2.0**HIGH)

    @pl.when(jnp.logical_not(fast))
    def _():
        slow_over_targets(yt_ref, xa_ref, None, sum_ref)
        send(pack(sum_ref[...] - math.log2(n_tgt)), part_ref)


def checked(totals, pot):
    top = jnp.max(pot)
    floor = jnp.exp2(jnp.minimum(jnp.maximum(top, 0.0), HIGH) + LOW)
    return (top <= HIGH) & (jnp.min(totals) >= floor)


def row_sums(first, change):
    return first + decode(change)


def over_sources(log_targets, n_parts, *refs):
    parts_refs, refs = refs[:n_parts], refs[n_parts:]
    e_ref, yt_ref, xa_ref, part_ref, *rows_ref, sum_ref, pot_ref, yt_buf, xa_buf = refs
    n_tgt, n_src = e_ref.shape
    n_blocks = n_src // LANES
    if n_parts == 1:
        rows = math.log2(n_tgt) + unpack(parts_refs[0][...])
        rows_ref[0][...] = rows
    else:
        rows = row_sums(*[ref[...] for ref in parts_refs])
    pot = log_targets - merge(rows)
    pot_ref[...] = pot
    u = jnp.exp2(jnp.minimum(pot, HIGH))
    u = [jnp.broadcast_to(u[b : b + 1], (8, LANES)) for b in range(n_blocks)]
    for k in range(n_tgt // LANES):
        block = []
        for r in range(k * LANES, (k + 1) * LANES, 8):
            acc = e_ref[r : r + 8, :LANES] * u[0]
            for b in range(1, n_blocks):
                acc = acc + e_ref[r : r + 8, b * LANES : (b + 1) * LANES] * u[b]
            block.append(acc)
        sum_ref[k : k + 1, :] = jnp.sum(jnp.concatenate(block, axis=0).T, axis=0, keepdims=True)
    totals = sum_ref[...]

    def put(value):
        copies, n, _ = part_ref.shape
        if part_ref.dtype == BF16:
            value = encode(value - math.log2(n_src))
        for k in range(copies):
            at = k * value.shape[0] // copies // n * n
            part_ref[k] = value[at : at + n]

    put(jnp.log2(totals))

    @pl.when(jnp.logical_not(checked(totals, pot)))
    def _():
        pltpu.sync_copy(yt_ref, yt_buf)
        pltpu.sync_copy(xa_ref, xa_buf)
        slow_over_sources(yt_buf, xa_buf, pot_ref, sum_ref)
        put(sum_ref[...])


def over_targets(log_sources, parts_ref, before_ref, e_ref, yt_ref, xa_ref, part_ref, sum_ref, pot_ref, yt_buf, xa_buf):
    n_tgt, n_src = e_ref.shape
    n_blocks = n_src // LANES
    pot = log_sources - merge(math.log2(n_src) + decode(parts_ref[...]))
    u = jnp.exp2(jnp.minimum(pot, HIGH))
    acc = [jnp.zeros((8, LANES), F32)] * n_blocks
    for k in range(n_tgt // LANES):
        v = jnp.broadcast_to(u[k : k + 1], (LANES, LANES)).T
        for r in range(0, LANES, 8):
            at = k * LANES + r
            for b in range(n_blocks):
                acc[b] = acc[b] + e_ref[at : at + 8, b * LANES : (b + 1) * LANES] * v[r : r + 8]
    for b in range(n_blocks):
        sum_ref[b : b + 1, :] = jnp.sum(acc[b], axis=0, keepdims=True)
    totals = sum_ref[...]
    before = math.log2(n_tgt) + unpack(before_ref[0])
    send(encode(jnp.log2(totals) - before), part_ref)

    @pl.when(jnp.logical_not(checked(totals, pot)))
    def _():
        pltpu.sync_copy(yt_ref, yt_buf)
        pltpu.sync_copy(xa_ref, xa_buf)
        spread_to_rows(pot, pot_ref)
        slow_over_targets(yt_buf, xa_buf, pot_ref, sum_ref)
        send(encode(sum_ref[...] - before), part_ref)


def make_copies(x_ref, out_ref, buf, sems):
    pltpu.sync_copy(x_ref, buf)
    copies = [pltpu.make_async_copy(buf, out_ref.at[k], sems.at[k]) for k in range(out_ref.shape[0])]
    for copy in copies:
        copy.start()
    for copy in copies:
        copy.wait()


def finish_sources(log_targets, first_ref, change_ref, out_ref):
    out_ref[...] = FROM_LOG2 * (log_targets - merge(row_sums(first_ref[...], change_ref[...])))


def finish_targets(log_sources, parts_ref, out_ref):
    out_ref[...] = FROM_LOG2 * (log_sources - merge(parts_ref[...]))


VMEM = pl.BlockSpec(memory_space=pltpu.VMEM)
ANY = pl.BlockSpec(memory_space=pl.ANY)
LIMIT = 20 << 20


def params():
    return pltpu.CompilerParams(vmem_limit_bytes=LIMIT)


def call_prep(y):
    cores, width, own = y.shape
    return pl.pallas_call(
        prep_targets,
        out_shape=jax.ShapeDtypeStruct((cores * own, 4 * width), BF16),
        in_specs=[VMEM],
        out_specs=VMEM,
        compiler_params=params(),
        name="prep_targets",
    )(y)


def call_copies(x, copies):
    return pl.pallas_call(
        make_copies,
        out_shape=pltpu.HBM((copies,) + x.shape, x.dtype),
        in_specs=[ANY],
        out_specs=ANY,
        scratch_shapes=[pltpu.VMEM(x.shape, x.dtype), pltpu.SemaphoreType.DMA((copies,))],
        compiler_params=params(),
        name="make_copies",
    )(pltpu.with_memory_space_constraint(x, pltpu.HBM))


def call_finish_sources(log_targets, first, change):
    return pl.pallas_call(
        functools.partial(finish_sources, log_targets),
        out_shape=jax.ShapeDtypeStruct(change.shape[1:], F32),
        in_specs=[VMEM, VMEM],
        out_specs=VMEM,
        compiler_params=params(),
        name="finish_sources",
    )(first, change)


def call_finish(log_sources, parts):
    return pl.pallas_call(
        functools.partial(finish_targets, log_sources),
        out_shape=jax.ShapeDtypeStruct(parts.shape[1:], F32),
        in_specs=[VMEM],
        out_specs=VMEM,
        compiler_params=params(),
        name="finish_targets",
    )(parts)


def call_first(yt, x, copies, tile=128):
    n_blocks, width, lanes = x.shape
    n_tgt, n_src = yt.shape[0], n_blocks * lanes
    return pl.pallas_call(
        functools.partial(first_over_targets, tile),
        out_shape=(
            pltpu.VMEM((n_tgt, n_src), F32),
            jax.ShapeDtypeStruct((4 * width, n_src), BF16),
            jax.ShapeDtypeStruct((copies, n_blocks + n_blocks // 2, lanes), BF16),
        ),
        in_specs=[VMEM, VMEM],
        out_specs=(VMEM, VMEM, VMEM),
        scratch_shapes=[pltpu.VMEM((n_blocks, lanes), F32)],
        compiler_params=params(),
        name="first_over_targets",
    )(yt, x)


def call_over_sources(log_targets, e, yt, xa, part_shape, part_type, *parts):
    n_tgt, n_src = e.shape
    out_shape = [jax.ShapeDtypeStruct(part_shape, part_type)]
    if len(parts) == 1:
        out_shape.append(jax.ShapeDtypeStruct((parts[0].shape[0], n_src // LANES, LANES), F32))
    return pl.pallas_call(
        functools.partial(over_sources, log_targets, len(parts)),
        out_shape=out_shape,
        in_specs=[VMEM] * len(parts) + [VMEM, ANY, ANY],
        out_specs=[VMEM] * len(out_shape),
        scratch_shapes=[
            pltpu.VMEM((n_tgt // LANES, LANES), F32),
            pltpu.VMEM((n_src // LANES, LANES), F32),
            pltpu.VMEM(yt.shape, BF16),
            pltpu.VMEM(xa.shape, BF16),
        ],
        compiler_params=params(),
        name="over_sources",
    )(*parts, e, yt, xa)


def call_over_targets(log_sources, parts, before, e, yt, xa, copies):
    n_tgt, n_src = e.shape
    return pl.pallas_call(
        functools.partial(over_targets, log_sources),
        out_shape=jax.ShapeDtypeStruct((copies, n_src // LANES, LANES), BF16),
        in_specs=[VMEM, VMEM, VMEM, ANY, ANY],
        out_specs=VMEM,
        scratch_shapes=[
            pltpu.VMEM((n_src // LANES, LANES), F32),
            pltpu.VMEM((n_tgt, LANES), F32),
            pltpu.VMEM(yt.shape, BF16),
            pltpu.VMEM(xa.shape, BF16),
        ],
        compiler_params=params(),
        name="over_targets",
    )(parts, before, e, yt, xa)


def exchange(value, axis):
    return lax.all_to_all(value, axis, 0, 0, tiled=False)


def per_device(n_row, n_z, n_core, src_feat, tgt_feat):
    width, src_own = src_feat.shape
    tgt_own = tgt_feat.shape[1]
    log_sources = math.log2(src_own * n_row * n_z * n_core)
    log_targets = math.log2(tgt_own * n_z * n_core)
    n_tgt = n_core * tgt_own
    group = n_row * n_core
    x = exchange(call_copies(src_feat, n_z), "z")
    yt = call_prep(lax.all_gather(tgt_feat, "core"))
    e, xa, part = call_first(yt, x, n_z)
    first = exchange(part, "z")
    col_part, first = call_over_sources(log_targets, e, yt, xa, (group, n_tgt // LANES, LANES), BF16, first)
    col_parts = exchange(col_part, ("core", "row"))
    change = exchange(call_over_targets(log_sources, col_parts, part, e, yt, xa, n_z), "z")
    (col_part,) = call_over_sources(log_targets, e, yt, xa, (group, tgt_own // LANES, LANES), F32, first, change)
    src_pot = call_finish_sources(log_targets, first, change)
    src_pot = lax.all_gather(src_pot, "core", axis=1)
    tgt_pot = call_finish(log_sources, exchange(col_part, ("core", "row")))
    return src_pot.reshape(n_core * n_z * src_own), tgt_pot.reshape(tgt_own)


def solution(mesh):
    n_row, n_col = mesh.shape["row"], mesh.shape["col"]
    n_core = 2
    n_z = n_col // n_core
    fine = Mesh(mesh.devices.reshape(n_row, n_z, n_core), ("row", "z", "core"))
    return jax.shard_map(
        functools.partial(per_device, n_row, n_z, n_core),
        mesh=fine,
        in_specs=(P(None, ("row", "z", "core")), P(None, ("z", "core"))),
        out_specs=(P("row"), P(("z", "core"))),
        check_vma=False,
    )
```
